512 devices in a mesh: dp: 16 (over y_hi, x, core), fsdp: 32 (over z, y_lo).
Axes of the slice: x: 4, y: 4 (y_hi: 2, y_lo: 2; y = y_hi * 2 + y_lo), z: 16, core: 2. Of those that a mesh axis runs over, the one named last changes fastest.
Arguments:
- attention_output_rows: bfloat16 [131072, 1536], P(('dp', 'fsdp')), may hold values from -24 to 24
- cotangent: bfloat16 [131072, 3072], P(('dp', 'fsdp')), may hold values from -24 to 24
- quantized_weight_codes: bfloat16 [1536, 3072], P('fsdp'), may hold values from -1 to 1
- shard_absolute_maximum: bfloat16 [32], P('fsdp'), may hold values from 0.019897461 to 0.079589844
- adapter_down_weight: bfloat16 [1536, 128], P('fsdp'), may hold values from -0.15625 to 0.15625
- adapter_up_weight: bfloat16 [128, 3072], P(None, 'fsdp'), may hold values from -0.5 to 0.5
- timestep_gate_weight: bfloat16 [256, 3072], P('fsdp'), may hold values from -0.375 to 0.375
- timesteps: int32 [32], replicated, may hold values from 0 to 999
Outputs:
- mixed_update: bfloat16 [131072, 3072], P(('dp', 'fsdp'))
- attention_output_gradient: bfloat16 [131072, 1536], P(('dp', 'fsdp'))
- down_grad: float32 [1536, 128], P('fsdp')
- scaled_up_gradient: float32 [128, 3072], P(None, 'fsdp')
The draws below stay inside these ranges and needn't reach their ends.
All inputs are finite; a program needn't handle non-finite values.
Results may differ from the reference program's by a relative error of at most 0.0075.
Values may be sent and summed in bfloat16 or wider, within the bound.
No kernel may reach another device: no remote copies, remote signals or barrier semaphores. Data moves between devices by JAX's collectives and lax.ppermute only.
A program may use at most 64 MiB of HBM per device.

```python
import math
import jax
import jax.numpy as jnp

MODEL_WIDTH = 3072
INNER_FEATURES = 1536
ADAPTER_RANK = 128
FREQ = 256
PATCHES = 4096
TOKENS = 131072
SAMPLES = 32
N_FSDP = 32


def plant(values, rng, smallest, top_value):
    longest = values.shape.index(max(values.shape))
    spots = []
    for shift in (0, 1):
        where = [jax.random.randint(jax.random.fold_in(rng, axis), (), 0, length) for axis, length in enumerate(values.shape)]
        where[longest] = (where[longest] + shift) % values.shape[longest]
        spots.append(tuple(where))
    return values.at[spots[0]].set(smallest).at[spots[1]].set(top_value)


def strengthened(values, own_key, source, target, blocks, factor):
    def block_of(axis_at):
        return (jnp.arange(values.shape[axis_at]) // (values.shape[axis_at] // blocks)).reshape((-1,) + (1,) * (values.ndim - 1 - axis_at))

    one_side = jax.random.permutation(own_key, blocks)[block_of(target)]
    far = (block_of(target) + blocks // 2) % blocks
    return jnp.where((block_of(source) == one_side) | (block_of(source) == far), factor * values, values)


def block_levels(stream_key, extent, cuts, smallest, largest):
    def one(position, parts):
        draws = jax.random.uniform(jax.random.fold_in(jax.random.fold_in(stream_key, 6), position), (parts,), jnp.float32, smallest / len(cuts), largest / len(cuts))
        return jnp.repeat(jnp.exp(draws), extent[position] // parts).reshape((-1,) + (1,) * (len(extent) - position - 1))

    gain = one(*cuts[0])
    for cut in cuts[1:]:
        gain = gain * one(*cut)
    return gain


def centred(rng, shape, spread, most, shards=(), kind=jnp.bfloat16):
    loudness = block_levels(rng, shape, shards, -0.22, 0.18) if shards else 1.0
    entries = jax.random.normal(rng, shape, jnp.float32) * spread * loudness
    return jnp.minimum(jnp.maximum(entries, -most), most).astype(kind)


def gaussian_with(rng, dims, spread, most, shards, heavy, kind=jnp.bfloat16):
    array = spread * jax.random.normal(rng, dims, jnp.float32)
    if shards:
        array = array * block_levels(rng, dims, shards, -0.22, 0.18)
    return jnp.clip(strengthened(array, jax.random.fold_in(rng, 3), *heavy), -most, most).astype(kind)


def setup_inputs(seed: int = 0) -> dict:
    splits = jax.random.split(jax.random.key(seed), 9)
    attention_output_rows = gaussian_with(splits[0], (TOKENS, INNER_FEATURES), 1.0, 24.0, ((0, 512),), (0, 1, 512, 6.0))
    cotangent = gaussian_with(splits[1], (TOKENS, MODEL_WIDTH), 1.0, 24.0, ((0, 512),), (0, 1, 512, 6.0))
    quantized_weight_codes = jnp.clip(jax.random.uniform(splits[2], (INNER_FEATURES, MODEL_WIDTH), jnp.float32, -1.0, 1.0) * block_levels(splits[2], (INNER_FEATURES, MODEL_WIDTH), ((0, 32),), -0.4, 0.0), -1.0, 1.0).astype(jnp.bfloat16)
    shard_absolute_maximum = jnp.clip(jnp.exp(math.log(0.079589844) - 1.3862944 * jax.random.uniform(splits[3], (N_FSDP,), jnp.float32) ** block_levels(splits[3], (N_FSDP,), ((0, 32),), -0.2, 0.2)), 0.019897461, 0.079589844).astype(jnp.bfloat16)
    adapter_down_weight = centred(splits[4], (INNER_FEATURES, ADAPTER_RANK), INNER_FEATURES ** -0.5, 0.15625, ((0, 32),))
    adapter_up_weight = centred(splits[5], (ADAPTER_RANK, MODEL_WIDTH), ADAPTER_RANK ** -0.5, 0.5, ((1, 32),))
    timestep_gate_weight = centred(splits[6], (FREQ, MODEL_WIDTH), FREQ ** -0.5, 0.375, ((0, 32),))
    timesteps = plant(jax.random.randint(splits[7], (SAMPLES,), 0, 1000), jax.random.fold_in(splits[7], 1), 0, 999).astype(jnp.int32)
    return dict(attention_output_rows=attention_output_rows, cotangent=cotangent, quantized_weight_codes=quantized_weight_codes, shard_absolute_maximum=shard_absolute_maximum, adapter_down_weight=adapter_down_weight, adapter_up_weight=adapter_up_weight, timestep_gate_weight=timestep_gate_weight, timesteps=timesteps)


adapter_scale_factor = 0.5


def reference(attention_output_rows, cotangent, quantized_weight_codes, shard_absolute_maximum, adapter_down_weight, adapter_up_weight, timestep_gate_weight, timesteps):
    shard_rows = INNER_FEATURES // N_FSDP
    amax_rows = jnp.repeat(shard_absolute_maximum.astype(jnp.float32), shard_rows)
    weight = (quantized_weight_codes.astype(jnp.float32) * amax_rows[:, None]).astype(jnp.bfloat16)
    half_freq = FREQ // 2
    frequency = jnp.exp(-math.log(10000.0) * jnp.arange(half_freq, dtype=jnp.float32) / half_freq)
    phase_angle = timesteps.astype(jnp.float32)[:, None] * frequency[None, :]
    features = jnp.concatenate([jnp.cos(phase_angle), jnp.sin(phase_angle)], axis=1).astype(jnp.bfloat16)
    gate_row = jnp.dot(features, timestep_gate_weight, preferred_element_type=jnp.float32)
    bottleneck_activation = jnp.dot(attention_output_rows, adapter_down_weight, preferred_element_type=jnp.float32).astype(jnp.bfloat16)
    projection_output = jnp.dot(attention_output_rows, weight, preferred_element_type=jnp.float32)
    projection_output = projection_output + adapter_scale_factor * jnp.dot(bottleneck_activation, adapter_up_weight, preferred_element_type=jnp.float32)
    mixed_update = (projection_output.reshape(SAMPLES, PATCHES, MODEL_WIDTH) * gate_row[:, None, :]).reshape(TOKENS, MODEL_WIDTH).astype(jnp.bfloat16)
    gated_branch_gradient = (cotangent.astype(jnp.float32).reshape(SAMPLES, PATCHES, MODEL_WIDTH) * gate_row[:, None, :]).reshape(TOKENS, MODEL_WIDTH).astype(jnp.bfloat16)
    bottleneck_gradient = (adapter_scale_factor * jnp.dot(gated_branch_gradient, adapter_up_weight.T, preferred_element_type=jnp.float32)).astype(jnp.bfloat16)
    attention_output_gradient = jnp.dot(gated_branch_gradient, weight.T, preferred_element_type=jnp.float32)
    attention_output_gradient = (attention_output_gradient + jnp.dot(bottleneck_gradient, adapter_down_weight.T, preferred_element_type=jnp.float32)).astype(jnp.bfloat16)
    gradient_scale_factor = TOKENS ** -0.5
    down_grad = jnp.dot(attention_output_rows.T, bottleneck_gradient, preferred_element_type=jnp.float32) * gradient_scale_factor
    scaled_up_gradient = jnp.dot(bottleneck_activation.T, gated_branch_gradient, preferred_element_type=jnp.float32) * (adapter_scale_factor * gradient_scale_factor)
    return mixed_update, attention_output_gradient, down_grad, scaled_up_gradient
```

```python
import math

import jax
import jax.numpy as jnp
from jax import lax
from jax.experimental import pallas as pl
from jax.experimental.pallas import tpu as pltpu
from jax.sharding import Mesh
from jax.sharding import PartitionSpec as P

FREQ = 256
SCALE = 0.5
AXES = ("yh", "x", "core", "z", "yl")
SIZES = (2, 4, 2, 16, 2)
PLANE = ("yh", "x", "yl")
BF = jnp.bfloat16
F32 = jnp.float32


def index_of(yh, x, c, z, yl):
    return (((yh * 4 + x) * 2 + c) * 16 + z) * 2 + yl


def plane_pairs(k, swap):
    pairs = []
    for yh in range(2):
        for x in range(4):
            for c in range(2):
                for z in range(16):
                    for yl in range(2):
                        tx, ty = x, yh * 2 + yl
                        if (c == 0) != swap:
                            tx ^= k
                        else:
                            ty ^= k
                        pairs.append((index_of(yh, x, c, z, yl), index_of(ty >> 1, tx, c, z, ty & 1)))
    return pairs


def other_core(v):
    return lax.ppermute(v, "core", [(0, 1), (1, 0)])


def assemble_kernel(at_ref, t0, t1, t2, t3, out_ref, sems):
    copies = []
    for k2, t in enumerate((t0, t1, t2, t3)):
        for k1 in range(4):
            b = k2 * 4 + k1
            col = pl.multiple_of(at_ref[b] * 384, 128)
            copy = pltpu.make_async_copy(
                t.at[k1], out_ref.at[:, at_ref[16 + b], :, pl.ds(col, 384)], sems.at[b]
            )
            copy.start()
            copies.append(copy)
    for copy in copies:
        copy.wait()


def assemble(at, blocks):
    hbm = pl.BlockSpec(memory_space=pl.ANY)
    return pl.pallas_call(
        assemble_kernel,
        out_shape=jax.ShapeDtypeStruct((16, 4, 24, 1536), BF),
        in_specs=[pl.BlockSpec(memory_space=pltpu.SMEM)] + [hbm] * 4,
        out_specs=hbm,
        scratch_shapes=[pltpu.SemaphoreType.DMA((16,))],
        name="assemble_weight",
    )(at, *blocks)


def per_device(rows, cotangent, codes, amax, down, up, gate_weight, timesteps):
    yh, xi, core, z, yl = (lax.axis_index(a) for a in AXES)
    j = yh * 4 + xi
    y = yh * 2 + yl

    upT = up.T
    down_piece = lax.dynamic_slice(down, (6 * j, 0), (6, 128))
    up_piece = lax.dynamic_slice(upT, (12 * j, 0), (12, 128))
    gate_piece = lax.dynamic_slice(gate_weight, (0, core * 1536 + j * 192), (8, 192)).reshape(12, 128)
    small = jnp.concatenate([down_piece, up_piece, gate_piece], axis=0)
    small = lax.all_to_all(jnp.broadcast_to(small[None], (16, 30, 128)), "z", 0, 0, tiled=True)

    weight = (codes.astype(F32) * amax.astype(F32)[0]).astype(BF)
    piece = lax.dynamic_slice(weight, (24 * yh, core * 1536 + xi * 384), (24, 384))
    line = lax.all_to_all(jnp.broadcast_to(piece[None], (16, 24, 384)), "z", 0, 0, tiled=True)
    first = jnp.stack([line] + [lax.ppermute(line, AXES, plane_pairs(k, False)) for k in (1, 2, 3)])
    second = [first] + [lax.ppermute(first, AXES, plane_pairs(k, True)) for k in (2, 1, 3)]
    second = [second[0], second[2], second[1], second[3]]
    k1 = jnp.tile(jnp.arange(4), 4)
    k2 = jnp.repeat(jnp.arange(4), 4)
    bx = xi ^ jnp.where(core == 0, k1, k2)
    by = y ^ jnp.where(core == 0, k2, k1)
    at = jnp.concatenate([bx, (by & 1) * 2 + (by >> 1)]).astype(jnp.int32)

    rows_other = other_core(rows)

    half_freq = FREQ // 2
    frequency = jnp.exp(-math.log(10000.0) * jnp.arange(half_freq, dtype=F32) / half_freq)
    steps = lax.dynamic_slice(timesteps.reshape(16, 2), (0, z // 8), (16, 1))
    phase = steps.astype(F32) * frequency[None, :]
    features = jnp.concatenate([jnp.cos(phase), jnp.sin(phase)], axis=1).astype(BF)
    features = lax.dynamic_slice(features.reshape(16, 16, 2, 8), (0, 0, yl, 0), (16, 16, 1, 8))
    gate_block = small[:, 18:].reshape(16, 8, 192).reshape(128, 192)
    part = jnp.dot(features.reshape(16, 128), gate_block, preferred_element_type=F32)
    high = lax.reduce_precision(part, 8, 7)
    pair = jnp.stack([high.astype(BF), (part - high).astype(BF)])
    pair = pair.reshape(2, 8, 2, 192).transpose(1, 0, 2, 3).reshape(8, 1, 6, 128)
    pair = jnp.broadcast_to(pair, (8, 2, 6, 128)).reshape(16, 6, 128)
    maps = jnp.broadcast_to(small[:, :18].reshape(1, 288, 128), (16, 288, 128))
    got = lax.all_to_all(jnp.concatenate([maps, pair], axis=1), PLANE, 0, 0, tiled=True)
    maps = got[:, :288].reshape(8, 2, 16, 18, 128).transpose(2, 1, 0, 3, 4)
    down_all = maps[:, :, :, :6].reshape(1536, 128)
    upT_all = maps[:, :, :, 6:].reshape(3072, 128)
    gates = got[:, 288:].reshape(8, 2, 2, 2, 192).astype(F32).sum((1, 2))
    gates = gates.transpose(1, 0, 2).reshape(2, 1536)
    gate_own = lax.dynamic_slice(gates, (core, 0), (1, 1536))
    gate_other = lax.dynamic_slice(gates, (1 - core, 0), (1, 1536))
    gate_rest = other_core(gate_other)
    gate_row = jnp.where(
        core == 0,
        jnp.concatenate([gate_own, gate_rest], axis=1),
        jnp.concatenate([gate_rest, gate_own], axis=1),
    )

    branch = (cotangent.astype(F32) * gate_row).astype(BF)
    branch_own = lax.dynamic_slice(branch, (0, core * 1536), (256, 1536))
    branch_other = other_core(lax.dynamic_slice(branch, (0, (1 - core) * 1536), (256, 1536)))
    low = jnp.dot(rows, down_all, preferred_element_type=F32).astype(BF)
    low_grad = (SCALE * jnp.dot(branch, upT_all, preferred_element_type=F32)).astype(BF)
    term_down = jnp.dot(rows.T, low_grad, preferred_element_type=F32).reshape(32, 2, 24, 128)
    term_up = jnp.dot(branch.T, low, preferred_element_type=F32).reshape(32, 2, 48, 128)
    terms = jnp.concatenate([term_down, term_up], axis=2)
    mine = lax.dynamic_slice(terms, (0, core, 0, 0), (32, 1, 72, 128))
    yours = lax.dynamic_slice(terms, (0, 1 - core, 0, 0), (32, 1, 72, 128))
    terms = (mine + other_core(yours)).astype(BF).reshape(16, 2, 8, 9, 128)
    terms = terms.transpose(2, 1, 0, 3, 4).reshape(16, 144, 128)
    terms = lax.all_to_all(terms, PLANE, 0, 0, tiled=True).astype(F32).sum(0).reshape(16, 9, 128)
    terms = lax.all_to_all(terms, "z", 0, 0, tiled=True).sum(0)
    terms = jnp.broadcast_to(terms[None], (16, 9, 128))
    terms = lax.all_to_all(terms, ("yh", "x", "core"), 0, 0, tiled=True)
    terms = terms.reshape(8, 2, 9, 128).transpose(1, 0, 2, 3).reshape(2, 72, 128)
    grad_scale = 131072**-0.5
    down_grad = terms[:, :24].reshape(48, 128) * grad_scale
    up_grad = terms[:, 24:].reshape(96, 128).T * (SCALE * grad_scale)

    low_other = jnp.dot(rows_other, down_all, preferred_element_type=F32).astype(BF)
    upT_half = lax.dynamic_slice(upT_all, (core * 1536, 0), (1536, 128))
    wm = assemble(at, second).reshape(1536, 1536)

    def back(b):
        return lax.dot_general(b, wm, (((1,), (1,)), ((), ())), preferred_element_type=F32)

    def forward(r, lo, g):
        p = jnp.dot(r, wm, preferred_element_type=F32)
        p = p + SCALE * lax.dot_general(lo, upT_half, (((1,), (1,)), ((), ())), preferred_element_type=F32)
        return (p * g).astype(BF)

    dx_rest = other_core(back(branch_other).astype(BF))
    mixed_rest = other_core(forward(rows_other, low_other, gate_other))
    mixed_own = forward(rows, low, gate_own)
    dx = back(branch_own) + lax.dot_general(
        low_grad, down_all, (((1,), (1,)), ((), ())), preferred_element_type=F32
    )
    dx = (dx + dx_rest.astype(F32)).astype(BF)
    mixed = jnp.where(
        core == 0,
        jnp.concatenate([mixed_own, mixed_rest], axis=1),
        jnp.concatenate([mixed_rest, mixed_own], axis=1),
    )
    return mixed, dx, down_grad, up_grad


def solution(mesh):
    fine = Mesh(mesh.devices.reshape(SIZES), AXES)
    dp, fsdp = ("yh", "x", "core"), ("z", "yl")
    every = dp + fsdp
    in_specs = (
        P(every, None),
        P(every, None),
        P(fsdp, None),
        P(fsdp),
        P(fsdp, None),
        P(None, fsdp),
        P(fsdp, None),
        P(),
    )
    out_specs = (P(every, None), P(every, None), P(fsdp, None), P(None, fsdp))
    return jax.shard_map(
        per_device, mesh=fine, in_specs=in_specs, out_specs=out_specs, check_vma=False
    )
```

```python
import math

import jax
import jax.numpy as jnp
from jax import lax
from jax.experimental import pallas as pl
from jax.experimental.pallas import tpu as pltpu
from jax.sharding import Mesh
from jax.sharding import PartitionSpec as P

FREQ = 256
SCALE = 0.5
AXES = ("yh", "x", "core", "z", "yl")
SIZES = (2, 4, 2, 16, 2)
PLANE = ("yh", "x", "yl")
BF = jnp.bfloat16
F32 = jnp.float32


def index_of(yh, x, c, z, yl):
    return (((yh * 4 + x) * 2 + c) * 16 + z) * 2 + yl


def plane_pairs(k, swap):
    pairs = []
    for yh in range(2):
        for x in range(4):
            for c in range(2):
                for z in range(16):
                    for yl in range(2):
                        tx, ty = x, yh * 2 + yl
                        if (c == 0) != swap:
                            tx ^= k
                        else:
                            ty ^= k
                        pairs.append((index_of(yh, x, c, z, yl), index_of(ty >> 1, tx, c, z, ty & 1)))
    return pairs


def other_core(v):
    return lax.ppermute(v, "core", [(0, 1), (1, 0)])


def nt(a, b):
    return lax.dot_general(a, b, (((1,), (1,)), ((), ())), preferred_element_type=F32)


def nn(a, b):
    return jnp.dot(a, b, preferred_element_type=F32)


STRIP = 256


def strips(body):
    def step(i, carry):
        body(pl.ds(pl.multiple_of(i * STRIP, STRIP), STRIP))
        return carry

    lax.fori_loop(0, 1536 // STRIP, step, 0)


def products(rows, branch, low, up, gate, wm, mixed, dx):
    def forward(s):
        p = nn(rows[...], wm[:, s]) + SCALE * nt(low[...], up[s, :])
        mixed[:, s] = (p * gate[:, s]).astype(BF)

    def back(s):
        dx[:, s] = nt(branch[...], wm[s, :]).astype(dx.dtype)

    strips(back)
    strips(forward)


def first_kernel(at, t0, t1, t2, t3, rows, branch, low, up, gate, wm, mixed, dx, blocks, sems):
    copies = []
    for k2, t in enumerate((t0, t1, t2, t3)):
        for k1 in range(4):
            b = k2 * 4 + k1
            col = pl.multiple_of(at[b] * 384, 128)
            copy = pltpu.make_async_copy(
                t.at[k1], blocks.at[:, at[16 + b], :, pl.ds(col, 384)], sems.at[b]
            )
            copy.start()
            copies.append(copy)
    for copy in copies:
        copy.wait()

    def pack(z, carry):
        part = blocks[z].astype(F32).reshape(96, 1536).astype(BF)
        wm[pl.ds(pl.multiple_of(z * 96, 96), 96), :] = part
        return carry

    lax.fori_loop(0, 16, pack, 0)
    products(rows, branch, low, up, gate, wm, mixed, dx)


def second_kernel(wm, rows, branch, low, up, gate, low_grad, down, mixed, dx):
    products(rows, branch, low, up, gate, wm, mixed, dx)

    def add(s):
        dx[:, s] = dx[:, s] + nt(low_grad[...], down[s, :])

    strips(add)


def vmem(n):
    return [pl.BlockSpec(memory_space=pltpu.VMEM)] * n


PARAMS = pltpu.CompilerParams(vmem_limit_bytes=48 * 1024 * 1024)
HALF = 256 * 1536 * 1536 * 2


def first_products(at, blocks, rows, branch, low, up, gate):
    return pl.pallas_call(
        first_kernel,
        out_shape=(
            jax.ShapeDtypeStruct((1536, 1536), BF),
            jax.ShapeDtypeStruct((256, 1536), BF),
            jax.ShapeDtypeStruct((256, 1536), BF),
        ),
        in_specs=[pl.BlockSpec(memory_space=pltpu.SMEM)]
        + [pl.BlockSpec(memory_space=pl.ANY)] * 4
        + vmem(5),
        out_specs=tuple(vmem(3)),
        scratch_shapes=[pltpu.VMEM((16, 4, 24, 1536), BF), pltpu.SemaphoreType.DMA((16,))],
        compiler_params=PARAMS,
        cost_estimate=pl.CostEstimate(flops=2 * HALF, bytes_accessed=13000000, transcendentals=0),
        name="other_rows",
    )(at, *blocks, rows, branch, low, up, gate)


def second_products(wm, rows, branch, low, up, gate, low_grad, down):
    return pl.pallas_call(
        second_kernel,
        out_shape=(
            jax.ShapeDtypeStruct((256, 1536), BF),
            jax.ShapeDtypeStruct((256, 1536), F32),
        ),
        in_specs=vmem(8),
        out_specs=tuple(vmem(2)),
        compiler_params=PARAMS,
        cost_estimate=pl.CostEstimate(flops=2 * HALF, bytes_accessed=10000000, transcendentals=0),
        name="own_rows",
    )(wm, rows, branch, low, up, gate, low_grad, down)


def per_device(rows, cotangent, codes, amax, down, up, gate_weight, timesteps):
    yh, xi, core, z, yl = (lax.axis_index(a) for a in AXES)
    j = yh * 4 + xi
    y = yh * 2 + yl

    upT = up.T
    down_piece = lax.dynamic_slice(down, (6 * j, 0), (6, 128))
    up_piece = lax.dynamic_slice(upT, (12 * j, 0), (12, 128))
    gate_piece = lax.dynamic_slice(gate_weight, (0, core * 1536 + j * 192), (8, 192)).reshape(12, 128)

    weight = (codes.astype(F32) * amax.astype(F32)[0]).astype(BF)
    piece = lax.dynamic_slice(weight, (24 * yh, core * 1536 + xi * 384), (24, 384))
    pieces = jnp.concatenate(
        [piece[:, :128], piece[:, 128:256], piece[:, 256:], down_piece, up_piece, gate_piece], axis=0
    )
    line = lax.all_to_all(jnp.broadcast_to(pieces[None], (16, 102, 128)), "z", 0, 0, tiled=True)
    small = line[:, 72:]
    line = jnp.concatenate([line[:, :24], line[:, 24:48], line[:, 48:72]], axis=2)
    first = jnp.stack([line] + [lax.ppermute(line, AXES, plane_pairs(k, False)) for k in (1, 2, 3)])
    second = [first] + [lax.ppermute(first, AXES, plane_pairs(k, True)) for k in (2, 1, 3)]
    second = [second[0], second[2], second[1], second[3]]
    k1 = jnp.tile(jnp.arange(4), 4)
    k2 = jnp.repeat(jnp.arange(4), 4)
    bx = xi ^ jnp.where(core == 0, k1, k2)
    by = y ^ jnp.where(core == 0, k2, k1)
    at = jnp.concatenate([bx, (by & 1) * 2 + (by >> 1)]).astype(jnp.int32)

    rows_other = other_core(rows)

    half_freq = FREQ // 2
    frequency = jnp.exp(-math.log(10000.0) * jnp.arange(half_freq, dtype=F32) / half_freq)
    steps = lax.dynamic_slice(timesteps.reshape(16, 2), (0, z // 8), (16, 1))
    phase = steps.astype(F32) * frequency[None, :]
    features = jnp.concatenate([jnp.cos(phase), jnp.sin(phase)], axis=1).astype(BF)
    features = lax.dynamic_slice(features.reshape(16, 16, 2, 8), (0, 0, yl, 0), (16, 16, 1, 8))
    gate_block = small[:, 18:].reshape(16, 8, 192).reshape(128, 192)
    part = jnp.dot(features.reshape(16, 128), gate_block, preferred_element_type=F32)
    high = lax.reduce_precision(part, 8, 7)
    pair = jnp.stack([high.astype(BF), (part - high).astype(BF)])
    pair = pair.reshape(2, 8, 2, 192).transpose(1, 0, 2, 3).reshape(8, 1, 6, 128)
    pair = jnp.broadcast_to(pair, (8, 2, 6, 128)).reshape(16, 6, 128)
    maps = jnp.broadcast_to(small[:, :18].reshape(1, 288, 128), (16, 288, 128))
    got = lax.all_to_all(jnp.concatenate([maps, pair], axis=1), PLANE, 0, 0, tiled=True)
    maps = got[:, :288].reshape(8, 2, 16, 18, 128).transpose(2, 1, 0, 3, 4)
    down_all = maps[:, :, :, :6].reshape(1536, 128)
    upT_all = maps[:, :, :, 6:].reshape(3072, 128)
    gates = got[:, 288:].reshape(8, 2, 2, 2, 192).astype(F32).sum((1, 2))
    gates = gates.transpose(1, 0, 2).reshape(2, 1536)
    gate_own = lax.dynamic_slice(gates, (core, 0), (1, 1536))
    gate_other = lax.dynamic_slice(gates, (1 - core, 0), (1, 1536))
    gate_rest = other_core(gate_other)
    gate_row = jnp.where(
        core == 0,
        jnp.concatenate([gate_own, gate_rest], axis=1),
        jnp.concatenate([gate_rest, gate_own], axis=1),
    )

    branch = (cotangent.astype(F32) * gate_row).astype(BF)
    branch_own = lax.dynamic_slice(branch, (0, core * 1536), (256, 1536))
    branch_other = other_core(lax.dynamic_slice(branch, (0, (1 - core) * 1536), (256, 1536)))
    low = jnp.dot(rows, down_all, preferred_element_type=F32).astype(BF)
    low_grad = (SCALE * jnp.dot(branch, upT_all, preferred_element_type=F32)).astype(BF)
    term_down = jnp.dot(rows.T, low_grad, preferred_element_type=F32).reshape(32, 2, 24, 128)
    term_up = jnp.dot(branch.T, low, preferred_element_type=F32).reshape(32, 2, 48, 128)
    terms = jnp.concatenate([term_down, term_up], axis=2)
    mine = lax.dynamic_slice(terms, (0, core, 0, 0), (32, 1, 72, 128))
    yours = lax.dynamic_slice(terms, (0, 1 - core, 0, 0), (32, 1, 72, 128))
    terms = (mine + other_core(yours)).astype(BF).reshape(32, 4, 18, 128)
    terms = lax.all_to_all(terms.transpose(1, 0, 2, 3), "x", 0, 0, tiled=True).astype(F32).sum(0)
    terms = terms.astype(BF).reshape(16, 36, 128)
    terms = lax.all_to_all(terms, "z", 0, 0, tiled=True).astype(F32).sum(0)
    terms = jnp.broadcast_to(terms.reshape(1, 2, 18, 128), (8, 2, 18, 128)).reshape(16, 18, 128)
    terms = lax.all_to_all(terms, PLANE, 0, 0, tiled=True)
    terms = terms.reshape(2, 4, 2, 18, 128).sum((0, 2)).reshape(72, 128)
    rest = other_core(terms)
    terms = jnp.stack([jnp.where(core == 0, terms, rest), jnp.where(core == 0, rest, terms)])
    grad_scale = 131072**-0.5
    down_grad = terms[:, :24].reshape(48, 128) * grad_scale
    up_grad = terms[:, 24:].reshape(96, 128).T * (SCALE * grad_scale)

    low_other = jnp.dot(rows_other, down_all, preferred_element_type=F32).astype(BF)
    upT_half = lax.dynamic_slice(upT_all, (core * 1536, 0), (1536, 128))
    wm, mixed_other, dx_other = first_products(
        at, second, rows_other, branch_other, low_other, upT_half, gate_other
    )
    dx_rest = other_core(dx_other)
    mixed_rest = other_core(mixed_other)
    mixed_own, dx = second_products(
        wm, rows, branch_own, low, upT_half, gate_own, low_grad, down_all
    )
    dx = (dx + dx_rest.astype(F32)).astype(BF)
    mixed = jnp.where(
        core == 0,
        jnp.concatenate([mixed_own, mixed_rest], axis=1),
        jnp.concatenate([mixed_rest, mixed_own], axis=1),
    )
    return mixed, dx, down_grad, up_grad


def solution(mesh):
    fine = Mesh(mesh.devices.reshape(SIZES), AXES)
    dp, fsdp = ("yh", "x", "core"), ("z", "yl")
    every = dp + fsdp
    in_specs = (
        P(every, None),
        P(every, None),
        P(fsdp, None),
        P(fsdp),
        P(fsdp, None),
        P(None, fsdp),
        P(fsdp, None),
        P(),
    )
    out_specs = (P(every, None), P(every, None), P(fsdp, None), P(None, fsdp))
    return jax.shard_map(
        per_device, mesh=fine, in_specs=in_specs, out_specs=out_specs, check_vma=False
    )
```

```python
import math

import jax
import jax.numpy as jnp
from jax import lax
from jax.experimental import pallas as pl
from jax.experimental.pallas import tpu as pltpu
from jax.sharding import Mesh
from jax.sharding import PartitionSpec as P

FREQ = 256
SCALE = 0.5
AXES = ("yh", "x", "core", "z", "yl")
SIZES = (2, 4, 2, 16, 2)
PLANE = ("yh", "x", "yl")
BF = jnp.bfloat16
F32 = jnp.float32


def index_of(yh, x, c, z, yl):
    return (((yh * 4 + x) * 2 + c) * 16 + z) * 2 + yl


def plane_pairs(k, swap):
    pairs = []
    for yh in range(2):
        for x in range(4):
            for c in range(2):
                for z in range(16):
                    for yl in range(2):
                        tx, ty = x, yh * 2 + yl
                        if (c == 0) != swap:
                            tx ^= k
                        else:
                            ty ^= k
                        pairs.append((index_of(yh, x, c, z, yl), index_of(ty >> 1, tx, c, z, ty & 1)))
    return pairs


def other_core(v):
    return lax.ppermute(v, "core", [(0, 1), (1, 0)])


def nt(a, b):
    return lax.dot_general(a, b, (((1,), (1,)), ((), ())), preferred_element_type=F32)


def nn(a, b):
    return jnp.dot(a, b, preferred_element_type=F32)


STRIPS = [slice(i, i + 256) for i in range(0, 1536, 256)]


def products_kernel(
    at, t0, t1, t2, t3, rows_other, branch_other, low_other, gate_other,
    rows, branch, low, gate, low_grad, up, down,
    mixed_other, dx_other, mixed, dx, blocks, wm, sems,
):
    copies = []
    for k2, t in enumerate((t0, t1, t2, t3)):
        for k1 in range(4):
            b = k2 * 4 + k1
            col = pl.multiple_of(at[b] * 384, 128)
            copy = pltpu.make_async_copy(
                t.at[k1], blocks.at[:, at[16 + b], :, pl.ds(col, 384)], sems.at[b]
            )
            copy.start()
            copies.append(copy)
    for copy in copies:
        copy.wait()

    def pack(z, carry):
        part = blocks[z].astype(F32).reshape(96, 1536).astype(BF)
        wm[pl.ds(pl.multiple_of(z * 96, 96), 96), :] = part
        return carry

    lax.fori_loop(0, 16, pack, 0)
    for s in STRIPS:
        dx_other[:, s] = nt(branch_other[...], wm[s, :]).astype(BF)
        dx[:, s] = nt(branch[...], wm[s, :]) + nt(low_grad[...], down[s, :])
    for s in STRIPS:
        p = nn(rows_other[...], wm[:, s]) + SCALE * nt(low_other[...], up[s, :])
        mixed_other[:, s] = (p * gate_other[:, s]).astype(BF)
        p = nn(rows[...], wm[:, s]) + SCALE * nt(low[...], up[s, :])
        mixed[:, s] = (p * gate[:, s]).astype(BF)


def finish_kernel(core, mixed_own, mixed_rest, dx_own, dx_rest, mixed, dx):
    own = pl.multiple_of(core[0] * 1536, 128)
    mixed[:, pl.ds(own, 1536)] = mixed_own[...]
    mixed[:, pl.ds(pl.multiple_of(1536 - own, 128), 1536)] = mixed_rest[...]
    dx[...] = (dx_own[...] + dx_rest[...].astype(F32)).astype(BF)


def vmem(n):
    return [pl.BlockSpec(memory_space=pltpu.VMEM)] * n


def adapter_kernel(
    core, got, rows, rows_other, cot,
    own, other, low, low_other, low_grad, down, up_half, gate_own, gate_other, mine, yours,
    wide, down_wide, up_wide, up, gates, branch, td, tu,
):
    for s in range(16):
        wide[s] = got[s].astype(F32)
        j, yl = s // 2, s % 2
        for z in range(16):
            a, b = 96 * z + 48 * yl + 6 * j, 192 * z + 96 * yl + 12 * j
            down_wide[a : a + 6] = wide[s, 18 * z : 18 * z + 6]
            up_wide[b : b + 12] = wide[s, 18 * z + 6 : 18 * z + 18]
    for j in range(8):
        part = wide[2 * j, 288:300] + wide[2 * j + 1, 288:300]
        part = part[:6] + part[6:]
        for r in range(6):
            at = 384 * j + 128 * (r % 3)
            gates[r // 3 : r // 3 + 1, at : at + 128] = part[r : r + 1]
    down[...] = down_wide[...].astype(BF)
    up[...] = up_wide[...].astype(BF)
    at = pl.multiple_of(core[0] * 1536, 128)
    rest = pl.multiple_of(1536 - at, 128)
    up_half[...] = up[pl.ds(at, 1536), :]
    first = core[0] == 0
    gate = jnp.where(first, gates[0:1], gates[1:2])
    gate_own[...] = jnp.where(first, gates[0:1, :1536], gates[1:2, 1536:])
    gate_other[...] = jnp.where(first, gates[1:2, :1536], gates[0:1, 1536:])

    branch[...] = (cot[...].astype(F32) * gate).astype(BF)
    own[...] = branch[:, pl.ds(at, 1536)]
    other[...] = branch[:, pl.ds(rest, 1536)]
    low_other[...] = nn(rows_other[...], down[...]).astype(BF)
    a = nn(rows[...], down[...]).astype(BF)
    low[...] = a
    b = (SCALE * nn(branch[...], up[...])).astype(BF)
    low_grad[...] = b
    a = a.astype(F32).T.astype(BF)
    b = b.astype(F32).T.astype(BF)
    for i in range(0, 1536, 384):
        td[i : i + 384, :] = nn(b, rows[:, i : i + 384]).T
    for i in range(0, 3072, 384):
        tu[i : i + 384, :] = nn(a, branch[:, i : i + 384]).T

    def put(h, ref):
        ref[:, :24] = td[...].reshape(32, 2, 24, 128)[:, h]
        ref[:, 24:] = tu[...].reshape(32, 2, 48, 128)[:, h]

    @pl.when(first)
    def _():
        put(0, mine)
        put(1, yours)

    @pl.when(jnp.logical_not(first))
    def _():
        put(1, mine)
        put(0, yours)


PARAMS = pltpu.CompilerParams(vmem_limit_bytes=28 * 1024 * 1024)
HALF = 256 * 1536 * 1536 * 2


def products(at, blocks, *args):
    half = jax.ShapeDtypeStruct((256, 1536), BF)
    return pl.pallas_call(
        products_kernel,
        out_shape=(half, half, half, jax.ShapeDtypeStruct((256, 1536), F32)),
        in_specs=[pl.BlockSpec(memory_space=pltpu.SMEM)]
        + [pl.BlockSpec(memory_space=pl.ANY)] * 4
        + vmem(11),
        out_specs=tuple(vmem(4)),
        scratch_shapes=[
            pltpu.VMEM((16, 4, 24, 1536), BF),
            pltpu.VMEM((1536, 1536), BF),
            pltpu.SemaphoreType.DMA((16,)),
        ],
        compiler_params=PARAMS,
        cost_estimate=pl.CostEstimate(flops=4 * HALF, bytes_accessed=12000000, transcendentals=0),
        name="products",
    )(at, *blocks, *args)


def finish(core, *args):
    return pl.pallas_call(
        finish_kernel,
        out_shape=(jax.ShapeDtypeStruct((256, 3072), BF), jax.ShapeDtypeStruct((256, 1536), BF)),
        in_specs=[pl.BlockSpec(memory_space=pltpu.SMEM)] + vmem(4),
        out_specs=tuple(vmem(2)),
        compiler_params=pltpu.CompilerParams(vmem_limit_bytes=16 * 1024 * 1024),
        cost_estimate=pl.CostEstimate(flops=1000000, bytes_accessed=7000000, transcendentals=0),
        name="finish",
    )(core.reshape(1), *args)


def adapter_terms(core, got, rows, rows_other, cot):
    def out(*shape):
        return jax.ShapeDtypeStruct(shape, BF)

    half, thin, row = out(256, 1536), out(256, 128), jax.ShapeDtypeStruct((1, 1536), F32)
    term = jax.ShapeDtypeStruct((32, 72, 128), F32)
    tall = out(1536, 128)
    return pl.pallas_call(
        adapter_kernel,
        out_shape=(half, half, thin, thin, thin, tall, tall, row, row, term, term),
        in_specs=[pl.BlockSpec(memory_space=pltpu.SMEM)] + vmem(4),
        out_specs=tuple(vmem(11)),
        scratch_shapes=[
            pltpu.VMEM((16, 300, 128), F32),
            pltpu.VMEM((1536, 128), F32),
            pltpu.VMEM((3072, 128), F32),
            pltpu.VMEM((3072, 128), BF),
            pltpu.VMEM((2, 3072), F32),
            pltpu.VMEM((256, 3072), BF),
            pltpu.VMEM((1536, 128), F32),
            pltpu.VMEM((3072, 128), F32),
        ],
        compiler_params=PARAMS,
        cost_estimate=pl.CostEstimate(flops=700000000, bytes_accessed=12000000, transcendentals=0),
        name="adapter_terms",
    )(core.reshape(1), got, rows, rows_other, cot)


def per_device(rows, cotangent, codes, amax, down, up, gate_weight, timesteps):
    yh, xi, core, z, yl = (lax.axis_index(a) for a in AXES)
    j = yh * 4 + xi
    y = yh * 2 + yl

    upT = up.T
    down_piece = lax.dynamic_slice(down, (6 * j, 0), (6, 128))
    up_piece = lax.dynamic_slice(upT, (12 * j, 0), (12, 128))
    gate_piece = lax.dynamic_slice(gate_weight, (0, j * 384), (8, 384)).reshape(24, 128)

    weight = (codes.astype(F32) * amax.astype(F32)[0]).astype(BF)
    piece = lax.dynamic_slice(weight, (24 * yh, core * 1536 + xi * 384), (24, 384))
    pieces = jnp.concatenate(
        [piece[:, :128], piece[:, 128:256], piece[:, 256:], down_piece, up_piece, gate_piece], axis=0
    )
    line = lax.all_to_all(jnp.broadcast_to(pieces[None], (16, 114, 128)), "z", 0, 0, tiled=True)
    line, rows_other = lax.optimization_barrier((line, other_core(rows)))
    small = line[:, 72:]
    line = jnp.concatenate([line[:, :24], line[:, 24:48], line[:, 48:72]], axis=2)
    first = jnp.stack([line] + [lax.ppermute(line, AXES, plane_pairs(k, False)) for k in (1, 2, 3)])
    k1 = jnp.tile(jnp.arange(4), 4)
    k2 = jnp.repeat(jnp.arange(4), 4)
    bx = xi ^ jnp.where(core == 0, k1, k2)
    by = y ^ jnp.where(core == 0, k2, k1)
    at = jnp.concatenate([bx, (by & 1) * 2 + (by >> 1)]).astype(jnp.int32)

    half_freq = FREQ // 2
    frequency = jnp.exp(-math.log(10000.0) * jnp.arange(half_freq, dtype=F32) / half_freq)
    steps = lax.dynamic_slice(timesteps.reshape(16, 2), (0, z // 8), (16, 1))
    phase = steps.astype(F32) * frequency[None, :]
    features = jnp.concatenate([jnp.cos(phase), jnp.sin(phase)], axis=1).astype(BF)
    features = lax.dynamic_slice(features.reshape(16, 16, 2, 8), (0, 0, yl, 0), (16, 16, 1, 8))
    gate_block = small[:, 18:].reshape(16, 8, 384).reshape(128, 384)
    part = jnp.dot(features.reshape(16, 128), gate_block, preferred_element_type=F32)
    high = lax.reduce_precision(part, 8, 7)
    pair = jnp.stack([high.astype(BF), (part - high).astype(BF)])
    pair = pair.reshape(2, 8, 2, 384).transpose(1, 0, 2, 3).reshape(8, 1, 12, 128)
    pair = jnp.broadcast_to(pair, (8, 2, 12, 128)).reshape(16, 12, 128)
    maps = jnp.broadcast_to(small[:, :18].reshape(1, 288, 128), (16, 288, 128))
    got = lax.all_to_all(jnp.concatenate([maps, pair], axis=1), PLANE, 0, 0, tiled=True)
    got, first = lax.optimization_barrier((got, first))
    second = [first] + [lax.ppermute(first, AXES, plane_pairs(k, True)) for k in (2, 1, 3)]
    second = [second[0], second[2], second[1], second[3]]

    (
        branch_own, branch_send, low, low_other, low_grad, down_all, up_half,
        gate_own, gate_other, mine, yours,
    ) = adapter_terms(core, got, rows, rows_other, cotangent)
    branch_other = other_core(branch_send)
    terms = (mine + other_core(yours)).astype(BF).reshape(16, 144, 128)
    terms, second[1] = lax.optimization_barrier((terms, second[1]))
    terms = lax.all_to_all(terms, "z", 0, 0, tiled=True).astype(F32).sum(0).astype(BF)

    mixed_other, dx_other, mixed_own, dx_own = products(
        at, second, rows_other, branch_other, low_other, gate_other,
        rows, branch_own, low, gate_own, low_grad, up_half, down_all,
    )
    dx_rest = other_core(dx_other)
    mixed_rest = other_core(mixed_other)
    dx_rest, mixed_rest, terms = lax.optimization_barrier((dx_rest, mixed_rest, terms))
    mixed, dx = finish(core, mixed_own, mixed_rest, dx_own, dx_rest)

    terms = jnp.broadcast_to(terms.reshape(1, 2, 72, 128), (8, 2, 72, 128)).reshape(16, 72, 128)
    terms = lax.all_to_all(terms, PLANE, 0, 0, tiled=True).astype(F32).sum(0)
    rest = other_core(terms)
    terms = jnp.stack([jnp.where(core == 0, terms, rest), jnp.where(core == 0, rest, terms)])
    grad_scale = 131072**-0.5
    down_grad = terms[:, :24].reshape(48, 128) * grad_scale
    up_grad = terms[:, 24:].reshape(96, 128).T * (SCALE * grad_scale)
    return mixed, dx, down_grad, up_grad


def solution(mesh):
    fine = Mesh(mesh.devices.reshape(SIZES), AXES)
    dp, fsdp = ("yh", "x", "core"), ("z", "yl")
    every = dp + fsdp
    in_specs = (
        P(every, None),
        P(every, None),
        P(fsdp, None),
        P(fsdp),
        P(fsdp, None),
        P(None, fsdp),
        P(fsdp, None),
        P(),
    )
    out_specs = (P(every, None), P(every, None), P(fsdp, None), P(None, fsdp))
    return jax.shard_map(
        per_device, mesh=fine, in_specs=in_specs, out_specs=out_specs, check_vma=False
    )
```

```python
import math

import jax
import jax.numpy as jnp
from jax import lax
from jax.experimental import pallas as pl
from jax.experimental.pallas import tpu as pltpu
from jax.sharding import Mesh
from jax.sharding import PartitionSpec as P

FREQ = 256
SCALE = 0.5
AXES = ("yh", "x", "core", "z", "yl")
SIZES = (2, 4, 2, 16, 2)
PLANE = ("yh", "x", "yl")
BF = jnp.bfloat16
F32 = jnp.float32


def index_of(yh, x, c, z, yl):
    return (((yh * 4 + x) * 2 + c) * 16 + z) * 2 + yl


def plane_pairs(k, swap):
    pairs = []
    for yh in range(2):
        for x in range(4):
            for c in range(2):
                for z in range(16):
                    for yl in range(2):
                        tx, ty = x, yh * 2 + yl
                        if (c == 0) != swap:
                            tx ^= k
                        else:
                            ty ^= k
                        pairs.append((index_of(yh, x, c, z, yl), index_of(ty >> 1, tx, c, z, ty & 1)))
    return pairs


def other_core(v):
    return lax.ppermute(v, "core", [(0, 1), (1, 0)])


def nt(a, b):
    return lax.dot_general(a, b, (((1,), (1,)), ((), ())), preferred_element_type=F32)


def nn(a, b):
    return jnp.dot(a, b, preferred_element_type=F32)


STRIPS = [slice(i, i + 256) for i in range(0, 1536, 256)]


def fetch(pairs, sems):
    copies = [pltpu.make_async_copy(a, b, sems.at[i]) for i, (a, b) in enumerate(pairs)]
    for copy in copies:
        copy.start()
    return copies


def products_kernel(
    at, core, low_other, gate_other, low, gate, low_grad,
    up_hbm, down_hbm, t0, t1, t2, t3, rows_hbm, rows_other_hbm, cot_hbm, cot_other_hbm,
    mixed_other_hbm, dx_other_hbm, mixed_hbm, dx_hbm,
    blocks, wm, rows, rows_other, cot, cot_other, branch, branch_other, up, down,
    mixed_other, dx_other, mixed, dx, sems,
):
    pairs = []
    for k2, t in enumerate((t0, t1, t2, t3)):
        for k1 in range(4):
            b = k2 * 4 + k1
            col = pl.multiple_of(at[b] * 384, 128)
            pairs.append((t.at[k1], blocks.at[:, at[16 + b], :, pl.ds(col, 384)]))
    half = pl.ds(pl.multiple_of(core[0] * 1536, 128), 1536)
    pairs.append((cot_other_hbm.at[:, half], cot_other))
    pairs.append((cot_hbm.at[:, half], cot))
    pairs.append((down_hbm, down))
    pairs.append((rows_other_hbm, rows_other))
    pairs.append((rows_hbm, rows))
    pairs.append((up_hbm, up))
    copies = fetch(pairs, sems)
    for copy in copies[:19]:
        copy.wait()
    branch_other[...] = (cot_other[...].astype(F32) * gate_other[...]).astype(BF)
    branch[...] = (cot[...].astype(F32) * gate[...]).astype(BF)

    def pack(z, carry):
        part = blocks[z].astype(F32).reshape(96, 1536).astype(BF)
        wm[pl.ds(pl.multiple_of(z * 96, 96), 96), :] = part
        return carry

    lax.fori_loop(0, 16, pack, 0)
    for s in STRIPS:
        dx_other[:, s] = nt(branch_other[...], wm[s, :]).astype(BF)
    out = fetch([(dx_other, dx_other_hbm)], sems.at[pl.ds(22, 1)])
    for copy in copies[19:]:
        copy.wait()
    for s in STRIPS:
        p = nn(rows_other[...], wm[:, s]) + SCALE * nt(low_other[...], up[s, :])
        mixed_other[:, s] = (p * gate_other[:, s]).astype(BF)
    out += fetch([(mixed_other, mixed_other_hbm)], sems.at[pl.ds(23, 1)])
    for s in STRIPS:
        dx[:, s] = nt(branch[...], wm[s, :]) + nt(low_grad[...], down[s, :])
    out += fetch([(dx, dx_hbm)], sems.at[pl.ds(24, 1)])
    for s in STRIPS:
        p = nn(rows[...], wm[:, s]) + SCALE * nt(low[...], up[s, :])
        mixed[:, s] = (p * gate[:, s]).astype(BF)
    out += fetch([(mixed, mixed_hbm.at[:, half])], sems.at[pl.ds(25, 1)])
    for copy in out:
        copy.wait()


def finish_kernel(
    core, mixed_in, mixed_rest_hbm, dx_own_hbm, dx_rest_hbm, mixed_hbm, dx_hbm,
    mixed_rest, dx_own, dx_rest, dx, sems,
):
    rest = pl.ds(pl.multiple_of(1536 - core[0] * 1536, 128), 1536)
    pairs = [(mixed_rest_hbm, mixed_rest), (dx_rest_hbm, dx_rest), (dx_own_hbm, dx_own)]
    copies = fetch(pairs, sems.at[pl.ds(0, 3)])
    copies[0].wait()
    out = fetch([(mixed_rest, mixed_hbm.at[:, rest])], sems.at[pl.ds(3, 1)])
    copies[1].wait()
    copies[2].wait()
    dx[...] = (dx_own[...] + dx_rest[...].astype(F32)).astype(BF)
    out += fetch([(dx, dx_hbm)], sems.at[pl.ds(4, 1)])
    for copy in out:
        copy.wait()


def vmem(n):
    return [pl.BlockSpec(memory_space=pltpu.VMEM)] * n


def adapter_kernel(
    core, got_hbm, rows_hbm, rows_other_hbm, cot_hbm, cot_other_hbm,
    low, low_other, low_grad, gate_own, gate_other, down_hbm, up_hbm, terms_hbm,
    wide, down_wide, up_wide, down, up, gates, branch, td, tu, kept, terms,
    rows, rows_other, cot, cot_other, got, sems,
):
    load = fetch([(got_hbm, got)], sems.at[pl.ds(7, 1)])
    copies = fetch(
        [(rows_hbm, rows), (rows_other_hbm, rows_other), (cot_hbm, cot), (cot_other_hbm, cot_other)],
        sems.at[pl.ds(0, 4)],
    )
    load[0].wait()
    for s in range(16):
        wide[s] = got[s].astype(F32)
        j, yl = s // 2, s % 2
        for z in range(16):
            a, b = 96 * z + 48 * yl + 6 * j, 192 * z + 96 * yl + 12 * j
            down_wide[a : a + 6] = wide[s, 18 * z : 18 * z + 6]
            up_wide[b : b + 12] = wide[s, 18 * z + 6 : 18 * z + 18]
    for j in range(8):
        part = wide[2 * j, 288:300] + wide[2 * j + 1, 288:300]
        part = part[:6] + part[6:]
        for r in range(6):
            at = 384 * j + 128 * (r % 3)
            gates[r // 3 : r // 3 + 1, at : at + 128] = part[r : r + 1]
    down[...] = down_wide[...].astype(BF)
    up[...] = up_wide[...].astype(BF)
    at = pl.multiple_of(core[0] * 1536, 128)
    out = fetch([(down, down_hbm), (up.at[pl.ds(at, 1536)], up_hbm)], sems.at[pl.ds(4, 2)])
    first = core[0] == 0
    gate = jnp.where(first, gates[0:1], gates[1:2])
    gate_own[...] = jnp.where(first, gates[0:1, :1536], gates[1:2, 1536:])
    gate_other[...] = jnp.where(first, gates[1:2, :1536], gates[0:1, 1536:])

    copies[0].wait()
    low[...] = nn(rows[...], down[...]).astype(BF)
    copies[1].wait()
    low_other[...] = nn(rows_other[...], down[...]).astype(BF)
    copies[2].wait()
    branch[:256] = (cot[...].astype(F32) * gate).astype(BF)
    b0 = (SCALE * nn(branch[:256], up[...])).astype(BF)
    low_grad[...] = b0
    copies[3].wait()
    branch[256:] = (cot_other[...].astype(F32) * jnp.where(first, gates[1:2], gates[0:1])).astype(BF)
    b1 = (SCALE * nn(branch[256:], up[...])).astype(BF)
    b0 = b0.astype(F32).T.astype(BF)
    b1 = b1.astype(F32).T.astype(BF)
    a0 = low[...].astype(F32).T.astype(BF)
    a1 = low_other[...].astype(F32).T.astype(BF)
    for i in range(0, 1536, 384):
        s = slice(i, i + 384)
        td[s, :] = (nn(b0, rows[:, s]) + nn(b1, rows_other[:, s])).T
    for i in range(0, 3072, 384):
        s = slice(i, i + 384)
        tu[s, :] = (nn(a0, branch[:256, s]) + nn(a1, branch[256:, s])).T

    def put(h):
        kept[:, :24] = td[...].reshape(32, 2, 24, 128)[:, h]
        kept[:, 24:] = tu[...].reshape(32, 2, 48, 128)[:, h]

    @pl.when(first)
    def _():
        put(0)

    @pl.when(jnp.logical_not(first))
    def _():
        put(1)

    terms[...] = kept[...].reshape(16, 144, 128).astype(BF)
    out += fetch([(terms, terms_hbm)], sems.at[pl.ds(6, 1)])
    for copy in out:
        copy.wait()


PARAMS = pltpu.CompilerParams(vmem_limit_bytes=60 * 1024 * 1024)
HALF = 256 * 1536 * 1536 * 2


def hbm(n):
    return [pl.BlockSpec(memory_space=pltpu.HBM)] * n


def products(at, core, *args):
    half = jax.ShapeDtypeStruct((256, 1536), BF)
    return pl.pallas_call(
        products_kernel,
        out_shape=(
            half,
            half,
            jax.ShapeDtypeStruct((256, 3072), BF),
            jax.ShapeDtypeStruct((256, 1536), F32),
        ),
        in_specs=[pl.BlockSpec(memory_space=pltpu.SMEM)] * 2 + vmem(5) + hbm(10),
        out_specs=tuple(hbm(4)),
        scratch_shapes=[
            pltpu.VMEM((16, 4, 24, 1536), BF),
            pltpu.VMEM((1536, 1536), BF),
            *[pltpu.VMEM((256, 1536), BF)] * 6,
            *[pltpu.VMEM((1536, 128), BF)] * 2,
            *[pltpu.VMEM((256, 1536), BF)] * 3,
            pltpu.VMEM((256, 1536), F32),
            pltpu.SemaphoreType.DMA((26,)),
        ],
        compiler_params=PARAMS,
        cost_estimate=pl.CostEstimate(flops=4 * HALF, bytes_accessed=200000000, transcendentals=0),
        name="products",
    )(at, core.reshape(1), *args)


def finish(core, *args):
    return pl.pallas_call(
        finish_kernel,
        out_shape=(jax.ShapeDtypeStruct((256, 3072), BF), jax.ShapeDtypeStruct((256, 1536), BF)),
        in_specs=[pl.BlockSpec(memory_space=pltpu.SMEM)] + hbm(4),
        out_specs=tuple(hbm(2)),
        input_output_aliases={1: 0},
        scratch_shapes=[
            pltpu.VMEM((256, 1536), BF),
            pltpu.VMEM((256, 1536), F32),
            *[pltpu.VMEM((256, 1536), BF)] * 2,
            pltpu.SemaphoreType.DMA((5,)),
        ],
        compiler_params=PARAMS,
        cost_estimate=pl.CostEstimate(flops=1000000, bytes_accessed=7000000, transcendentals=0),
        name="finish",
    )(core.reshape(1), *args)


def adapter_terms(core, *args):
    def out(*shape):
        return jax.ShapeDtypeStruct(shape, BF)

    thin, row = out(256, 128), jax.ShapeDtypeStruct((1, 1536), F32)
    tall = out(1536, 128)
    return pl.pallas_call(
        adapter_kernel,
        out_shape=(thin, thin, thin, row, row, tall, tall, out(16, 144, 128)),
        in_specs=[pl.BlockSpec(memory_space=pltpu.SMEM)] + hbm(5),
        out_specs=tuple(vmem(5) + hbm(3)),
        scratch_shapes=[
            pltpu.VMEM((16, 300, 128), F32),
            pltpu.VMEM((1536, 128), F32),
            pltpu.VMEM((3072, 128), F32),
            pltpu.VMEM((1536, 128), BF),
            pltpu.VMEM((3072, 128), BF),
            pltpu.VMEM((2, 3072), F32),
            pltpu.VMEM((512, 3072), BF),
            pltpu.VMEM((1536, 128), F32),
            pltpu.VMEM((3072, 128), F32),
            pltpu.VMEM((32, 72, 128), F32),
            pltpu.VMEM((16, 144, 128), BF),
            *[pltpu.VMEM((256, 1536), BF)] * 2,
            *[pltpu.VMEM((256, 3072), BF)] * 2,
            pltpu.VMEM((16, 300, 128), BF),
            pltpu.SemaphoreType.DMA((8,)),
        ],
        compiler_params=PARAMS,
        cost_estimate=pl.CostEstimate(flops=1400000000, bytes_accessed=200000000, transcendentals=0),
        name="adapter_terms",
    )(core.reshape(1), *args)


def pieces_kernel(at, codes, amax, down, up, gate, out, wide):
    core, xi, yh = at[0], at[1], at[2]
    j = yh * 4 + xi
    col = pl.multiple_of(core * 1536 + xi * 384, 128)
    weight = codes[:, pl.ds(col, 384)].astype(F32) * amax[...].astype(F32)
    weight = jnp.where(yh == 0, weight[:24], weight[24:]).astype(BF).astype(F32)
    gates = gate[:, pl.ds(pl.multiple_of(j * 384, 128), 384)].astype(F32)
    for k in range(3):
        lanes = slice(128 * k, 128 * k + 128)
        wide[24 * k : 24 * k + 24] = weight[:, lanes]
        wide[72 + 8 * k : 80 + 8 * k] = gates[:, lanes]

    def pick(n, size):
        row = lax.broadcasted_iota(jnp.int32, (n, size), 0)
        col = lax.broadcasted_iota(jnp.int32, (n, size), 1)
        return jnp.where(col == row + n * j, 1.0, 0.0).astype(BF)

    wide[96:102] = nn(pick(6, 48), down[...])
    wide[102:114] = nn(pick(12, 96), up[...])
    for d in range(16):
        out[d] = wide[...].astype(BF)


def pieces(at, codes, amax, down, up, gate):
    return pl.pallas_call(
        pieces_kernel,
        out_shape=jax.ShapeDtypeStruct((16, 114, 128), BF),
        in_specs=[pl.BlockSpec(memory_space=pltpu.SMEM)] + vmem(5),
        out_specs=vmem(1)[0],
        scratch_shapes=[pltpu.VMEM((114, 128), F32)],
        compiler_params=PARAMS,
        name="pieces",
    )(at, codes, amax, down, up, gate)


def spread_kernel(line, features, out_hbm, weight_hbm, wide, maps, pair, out, weight, sems):
    for k in range(3):
        weight[:, :, 128 * k : 128 * k + 128] = line[:, 24 * k : 24 * k + 24]
    copies = fetch([(weight, weight_hbm)], sems.at[pl.ds(0, 1)])
    wide[...] = line[...].astype(F32)
    for z in range(16):
        maps[18 * z : 18 * z + 18] = wide[z, 96:114]
    for k in range(3):
        block = wide[:, 72 + 8 * k : 80 + 8 * k].reshape(128, 128).astype(BF)
        part = nn(features[...], block)
        high = part.astype(BF).astype(F32)
        for h, v in enumerate((high, part - high)):
            for c in range(2):
                for j in range(8):
                    r = 6 * h + 3 * c + k
                    row = v[2 * j + c : 2 * j + c + 1]
                    pair[2 * j, r : r + 1] = row
                    pair[2 * j + 1, r : r + 1] = row
    for d in range(16):
        out[d, :288] = maps[...].astype(BF)
        out[d, 288:] = pair[d].astype(BF)
    copies += fetch([(out, out_hbm)], sems.at[pl.ds(1, 1)])
    for copy in copies:
        copy.wait()


def spread(line, features):
    shapes = ((16, 114, 128), (16, 300, 128), (16, 24, 384))
    return pl.pallas_call(
        spread_kernel,
        out_shape=tuple(jax.ShapeDtypeStruct(s, BF) for s in shapes[1:]),
        in_specs=vmem(2),
        out_specs=tuple(hbm(2)),
        scratch_shapes=[
            pltpu.VMEM(shapes[0], F32),
            pltpu.VMEM((288, 128), F32),
            pltpu.VMEM((16, 12, 128), F32),
            pltpu.VMEM(shapes[1], BF),
            pltpu.VMEM(shapes[2], BF),
            pltpu.SemaphoreType.DMA((2,)),
        ],
        compiler_params=pltpu.CompilerParams(vmem_limit_bytes=14 * 1024 * 1024),
        cost_estimate=pl.CostEstimate(flops=20000000, bytes_accessed=2000000, transcendentals=0),
        name="spread",
    )(line, features)


def per_device(rows, cotangent, codes, amax, down, up, gate_weight, timesteps):
    yh, xi, core, z, yl = (lax.axis_index(a) for a in AXES)
    j = yh * 4 + xi
    y = yh * 2 + yl

    place = jnp.stack([core, xi, yh]).astype(jnp.int32)
    line = pieces(place, codes, amax.reshape(1, 1), down, up.T, gate_weight)
    line = lax.all_to_all(line, "z", 0, 0, tiled=True)
    line, rows_other, cot_other = lax.optimization_barrier(
        (line, other_core(rows), other_core(cotangent))
    )
    k1 = jnp.tile(jnp.arange(4), 4)
    k2 = jnp.repeat(jnp.arange(4), 4)
    bx = xi ^ jnp.where(core == 0, k1, k2)
    by = y ^ jnp.where(core == 0, k2, k1)
    at = jnp.concatenate([bx, (by & 1) * 2 + (by >> 1)]).astype(jnp.int32)

    half_freq = FREQ // 2
    frequency = jnp.exp(-math.log(10000.0) * jnp.arange(half_freq, dtype=F32) / half_freq)
    steps = lax.dynamic_slice(timesteps.reshape(16, 2), (0, z // 8), (16, 1))
    phase = steps.astype(F32) * frequency[None, :]
    features = jnp.concatenate([jnp.cos(phase), jnp.sin(phase)], axis=1).astype(BF)
    features = lax.dynamic_slice(features.reshape(16, 16, 2, 8), (0, 0, yl, 0), (16, 16, 1, 8))
    spread_out, line = spread(line, features.reshape(16, 128))
    got = lax.all_to_all(spread_out, PLANE, 0, 0, tiled=True)
    first = [line] + [lax.ppermute(line, AXES, plane_pairs(k, False)) for k in (1, 2, 3)]
    got, first = lax.optimization_barrier((got, first))
    first = jnp.stack(first)
    second = [first] + [lax.ppermute(first, AXES, plane_pairs(k, True)) for k in (2, 1, 3)]
    second = [second[0], second[2], second[1], second[3]]

    low, low_other, low_grad, gate_own, gate_other, down_all, up_half, terms = adapter_terms(
        core, got, rows, rows_other, cotangent, cot_other
    )
    terms = lax.all_to_all(terms, "z", 0, 0, tiled=True)
    terms = terms.astype(F32).sum(0).astype(BF)

    mixed_other, dx_other, mixed_own, dx_own = products(
        at, core, low_other, gate_other, low, gate_own, low_grad,
        up_half, down_all, *second, rows, rows_other, cotangent, cot_other,
    )
    dx_rest = other_core(dx_other)
    mixed_rest = other_core(mixed_other)
    mixed, dx = finish(core, mixed_own, mixed_rest, dx_own, dx_rest)
    mixed, dx, terms = lax.optimization_barrier((mixed, dx, terms))
    terms = jnp.broadcast_to(terms.reshape(1, 2, 72, 128), (8, 2, 72, 128)).reshape(16, 72, 128)
    terms = lax.all_to_all(terms, PLANE, 0, 0, tiled=True).astype(F32).sum(0)
    rest = other_core(terms)
    terms = jnp.stack([jnp.where(core == 0, terms, rest), jnp.where(core == 0, rest, terms)])
    grad_scale = 131072**-0.5
    down_grad = terms[:, :24].reshape(48, 128) * grad_scale
    up_grad = terms[:, 24:].reshape(96, 128).T * (SCALE * grad_scale)
    return mixed, dx, down_grad, up_grad


def solution(mesh):
    fine = Mesh(mesh.devices.reshape(SIZES), AXES)
    dp, fsdp = ("yh", "x", "core"), ("z", "yl")
    every = dp + fsdp
    in_specs = (
        P(every, None),
        P(every, None),
        P(fsdp, None),
        P(fsdp),
        P(fsdp, None),
        P(None, fsdp),
        P(fsdp, None),
        P(),
    )
    out_specs = (P(every, None), P(every, None), P(fsdp, None), P(None, fsdp))
    return jax.shard_map(
        per_device, mesh=fine, in_specs=in_specs, out_specs=out_specs, check_vma=False
    )
```

```python
import math

import jax
import jax.numpy as jnp
from jax import lax
from jax.experimental import pallas as pl
from jax.experimental.pallas import tpu as pltpu
from jax.sharding import Mesh
from jax.sharding import PartitionSpec as P

FREQ = 256
SCALE = 0.5
AXES = ("yh", "x", "core", "z", "yl")
SIZES = (2, 4, 2, 16, 2)
PLANE = ("yh", "x", "yl")
BF = jnp.bfloat16
F32 = jnp.float32


def index_of(yh, x, c, z, yl):
    return (((yh * 4 + x) * 2 + c) * 16 + z) * 2 + yl


def plane_pairs(k, swap):
    pairs = []
    for yh in range(2):
        for x in range(4):
            for c in range(2):
                for z in range(16):
                    for yl in range(2):
                        tx, ty = x, yh * 2 + yl
                        if (c == 0) != swap:
                            tx ^= k
                        else:
                            ty ^= k
                        pairs.append((index_of(yh, x, c, z, yl), index_of(ty >> 1, tx, c, z, ty & 1)))
    return pairs


def other_core(v):
    return lax.ppermute(v, "core", [(0, 1), (1, 0)])


def nt(a, b):
    return lax.dot_general(a, b, (((1,), (1,)), ((), ())), preferred_element_type=F32)


def nn(a, b):
    return jnp.dot(a, b, preferred_element_type=F32)


STRIPS = [slice(i, i + 256) for i in range(0, 1536, 256)]


def fetch(pairs, sems):
    copies = [pltpu.make_async_copy(a, b, sems.at[i]) for i, (a, b) in enumerate(pairs)]
    for copy in copies:
        copy.start()
    return copies


def products_kernel(
    at, core, low_other, gate_other, low, gate, low_grad,
    up_hbm, down_hbm, t0, t1, t2, t3, rows_hbm, rows_other_hbm, cot_hbm, cot_other_hbm,
    mixed_other_hbm, dx_other_hbm, mixed_hbm, dx_hbm,
    blocks, wm, rows, rows_other, cot, cot_other, branch, branch_other, up, down,
    mixed_other, dx_other, mixed, dx, side_other, side, sems,
):
    half = pl.ds(pl.multiple_of(core[0] * 1536, 128), 1536)
    pairs = [(cot_other_hbm.at[:, half], cot_other), (cot_hbm.at[:, half], cot)]
    pairs += [(down_hbm, down), (up_hbm, up)]
    for k2, t in enumerate((t0, t1, t2, t3)):
        for k1 in range(4):
            b = k2 * 4 + k1
            col = pl.multiple_of(at[b] * 384, 128)
            pairs.append((t.at[k1], blocks.at[:, at[16 + b], :, pl.ds(col, 384)]))
    pairs += [(rows_other_hbm, rows_other), (rows_hbm, rows)]
    copies = fetch(pairs, sems)
    for copy in copies[:4]:
        copy.wait()
    branch_other[...] = (cot_other[...].astype(F32) * gate_other[...]).astype(BF)
    branch[...] = (cot[...].astype(F32) * gate[...]).astype(BF)
    for s in STRIPS:
        dx[:, s] = nt(low_grad[...], down[s, :])
        side_other[:, s] = SCALE * nt(low_other[...], up[s, :])
        side[:, s] = SCALE * nt(low[...], up[s, :])
    for copy in copies[4:20]:
        copy.wait()

    def pack(z, carry):
        part = blocks[z].astype(F32).reshape(96, 1536).astype(BF)
        wm[pl.ds(pl.multiple_of(z * 96, 96), 96), :] = part
        return carry

    lax.fori_loop(0, 16, pack, 0)
    for s in STRIPS:
        dx_other[:, s] = nt(branch_other[...], wm[s, :]).astype(BF)
    out = fetch([(dx_other, dx_other_hbm)], sems.at[pl.ds(22, 1)])
    for copy in copies[20:]:
        copy.wait()
    for s in STRIPS:
        p = nn(rows_other[...], wm[:, s]) + side_other[:, s]
        mixed_other[:, s] = (p * gate_other[:, s]).astype(BF)
    out += fetch([(mixed_other, mixed_other_hbm)], sems.at[pl.ds(23, 1)])
    for s in STRIPS:
        dx[:, s] = nt(branch[...], wm[s, :]) + dx[:, s]
    out += fetch([(dx, dx_hbm)], sems.at[pl.ds(24, 1)])
    for s in STRIPS:
        p = nn(rows[...], wm[:, s]) + side[:, s]
        mixed[:, s] = (p * gate[:, s]).astype(BF)
    out += fetch([(mixed, mixed_hbm.at[:, half])], sems.at[pl.ds(25, 1)])
    for copy in out:
        copy.wait()


def finish_kernel(
    core, mixed_in, mixed_rest_hbm, dx_own_hbm, dx_rest_hbm, mixed_hbm, dx_hbm,
    mixed_rest, dx_own, dx_rest, dx, sems,
):
    rest = pl.ds(pl.multiple_of(1536 - core[0] * 1536, 128), 1536)
    pairs = [(mixed_rest_hbm, mixed_rest), (dx_rest_hbm, dx_rest), (dx_own_hbm, dx_own)]
    copies = fetch(pairs, sems.at[pl.ds(0, 3)])
    copies[0].wait()
    out = fetch([(mixed_rest, mixed_hbm.at[:, rest])], sems.at[pl.ds(3, 1)])
    copies[1].wait()
    copies[2].wait()
    dx[...] = (dx_own[...] + dx_rest[...].astype(F32)).astype(BF)
    out += fetch([(dx, dx_hbm)], sems.at[pl.ds(4, 1)])
    for copy in out:
        copy.wait()


def vmem(n):
    return [pl.BlockSpec(memory_space=pltpu.VMEM)] * n


def adapter_kernel(
    core, got_hbm, got_other_hbm, rows_hbm, rows_other_hbm, cot_hbm, cot_other_hbm,
    low, low_other, low_grad, gate_own, gate_other, down_hbm, up_hbm, terms_hbm,
    wide, parts, down_wide, up_wide, down, up, gates, branch, td, tu, kept, terms,
    rows, rows_other, cot, cot_other, got, got_other, sems,
):
    load = fetch([(got_hbm, got), (got_other_hbm, got_other)], sems.at[pl.ds(7, 2)])
    copies = fetch(
        [(rows_hbm, rows), (rows_other_hbm, rows_other), (cot_hbm, cot), (cot_other_hbm, cot_other)],
        sems.at[pl.ds(0, 4)],
    )
    for copy in load:
        copy.wait()
    first = core[0] == 0
    for s in range(16):
        mine, theirs = got[s].astype(F32), got_other[s].astype(F32)
        wide[s] = mine
        parts[0] = jnp.where(first, mine, theirs)
        parts[1] = jnp.where(first, theirs, mine)
        j, yl = s // 2, s % 2
        for c in range(2):
            for z in range(16):
                a, b = 96 * z + 48 * yl + 6 * j + 3 * c, 192 * z + 96 * yl + 12 * j + 6 * c
                down_wide[a : a + 3] = parts[c, 9 * z : 9 * z + 3]
                up_wide[b : b + 6] = parts[c, 9 * z + 3 : 9 * z + 9]
    for j in range(8):
        part = wide[2 * j, 144:156] + wide[2 * j + 1, 144:156]
        part = part[:6] + part[6:]
        for r in range(6):
            at = 384 * j + 128 * (r % 3)
            gates[r // 3 : r // 3 + 1, at : at + 128] = part[r : r + 1]
    down[...] = down_wide[...].astype(BF)
    up[...] = up_wide[...].astype(BF)
    at = pl.multiple_of(core[0] * 1536, 128)
    out = fetch([(down, down_hbm), (up.at[pl.ds(at, 1536)], up_hbm)], sems.at[pl.ds(4, 2)])
    gate = jnp.where(first, gates[0:1], gates[1:2])
    gate_own[...] = jnp.where(first, gates[0:1, :1536], gates[1:2, 1536:])
    gate_other[...] = jnp.where(first, gates[1:2, :1536], gates[0:1, 1536:])

    copies[0].wait()
    low[...] = nn(rows[...], down[...]).astype(BF)
    copies[1].wait()
    low_other[...] = nn(rows_other[...], down[...]).astype(BF)
    copies[2].wait()
    branch[:256] = (cot[...].astype(F32) * gate).astype(BF)
    b0 = (SCALE * nn(branch[:256], up[...])).astype(BF)
    low_grad[...] = b0
    copies[3].wait()
    branch[256:] = (cot_other[...].astype(F32) * jnp.where(first, gates[1:2], gates[0:1])).astype(BF)
    b1 = (SCALE * nn(branch[256:], up[...])).astype(BF)
    b0 = b0.astype(F32).T.astype(BF)
    b1 = b1.astype(F32).T.astype(BF)
    a0 = low[...].astype(F32).T.astype(BF)
    a1 = low_other[...].astype(F32).T.astype(BF)
    for i in range(0, 1536, 384):
        s = slice(i, i + 384)
        td[s, :] = (nn(b0, rows[:, s]) + nn(b1, rows_other[:, s])).T
    for i in range(0, 3072, 384):
        s = slice(i, i + 384)
        tu[s, :] = (nn(a0, branch[:256, s]) + nn(a1, branch[256:, s])).T

    def put(h):
        kept[:, :24] = td[...].reshape(32, 2, 24, 128)[:, h]
        kept[:, 24:] = tu[...].reshape(32, 2, 48, 128)[:, h]

    @pl.when(first)
    def _():
        put(0)

    @pl.when(jnp.logical_not(first))
    def _():
        put(1)

    terms[...] = kept[...].reshape(16, 144, 128).astype(BF)
    out += fetch([(terms, terms_hbm)], sems.at[pl.ds(6, 1)])
    for copy in out:
        copy.wait()


PARAMS = pltpu.CompilerParams(vmem_limit_bytes=60 * 1024 * 1024)
HALF = 256 * 1536 * 1536 * 2


def hbm(n):
    return [pl.BlockSpec(memory_space=pltpu.HBM)] * n


def products(at, core, *args):
    half = jax.ShapeDtypeStruct((256, 1536), BF)
    return pl.pallas_call(
        products_kernel,
        out_shape=(
            half,
            half,
            jax.ShapeDtypeStruct((256, 3072), BF),
            jax.ShapeDtypeStruct((256, 1536), F32),
        ),
        in_specs=[pl.BlockSpec(memory_space=pltpu.SMEM)] * 2 + vmem(5) + hbm(10),
        out_specs=tuple(hbm(4)),
        scratch_shapes=[
            pltpu.VMEM((16, 4, 24, 1536), BF),
            pltpu.VMEM((1536, 1536), BF),
            *[pltpu.VMEM((256, 1536), BF)] * 6,
            *[pltpu.VMEM((1536, 128), BF)] * 2,
            *[pltpu.VMEM((256, 1536), BF)] * 3,
            *[pltpu.VMEM((256, 1536), F32)] * 3,
            pltpu.SemaphoreType.DMA((26,)),
        ],
        compiler_params=PARAMS,
        cost_estimate=pl.CostEstimate(flops=4 * HALF, bytes_accessed=200000000, transcendentals=0),
        name="products",
    )(at, core.reshape(1), *args)


def finish(core, *args):
    return pl.pallas_call(
        finish_kernel,
        out_shape=(jax.ShapeDtypeStruct((256, 3072), BF), jax.ShapeDtypeStruct((256, 1536), BF)),
        in_specs=[pl.BlockSpec(memory_space=pltpu.SMEM)] + hbm(4),
        out_specs=tuple(hbm(2)),
        input_output_aliases={1: 0},
        scratch_shapes=[
            pltpu.VMEM((256, 1536), BF),
            pltpu.VMEM((256, 1536), F32),
            *[pltpu.VMEM((256, 1536), BF)] * 2,
            pltpu.SemaphoreType.DMA((5,)),
        ],
        compiler_params=PARAMS,
        cost_estimate=pl.CostEstimate(flops=1000000, bytes_accessed=7000000, transcendentals=0),
        name="finish",
    )(core.reshape(1), *args)


def adapter_terms(core, *args):
    def out(*shape):
        return jax.ShapeDtypeStruct(shape, BF)

    thin, row = out(256, 128), jax.ShapeDtypeStruct((1, 1536), F32)
    tall = out(1536, 128)
    return pl.pallas_call(
        adapter_kernel,
        out_shape=(thin, thin, thin, row, row, tall, tall, out(16, 144, 128)),
        in_specs=[pl.BlockSpec(memory_space=pltpu.SMEM)] + hbm(6),
        out_specs=tuple(vmem(5) + hbm(3)),
        scratch_shapes=[
            pltpu.VMEM((16, 156, 128), F32),
            pltpu.VMEM((2, 156, 128), F32),
            pltpu.VMEM((1536, 128), F32),
            pltpu.VMEM((3072, 128), F32),
            pltpu.VMEM((1536, 128), BF),
            pltpu.VMEM((3072, 128), BF),
            pltpu.VMEM((2, 3072), F32),
            pltpu.VMEM((512, 3072), BF),
            pltpu.VMEM((1536, 128), F32),
            pltpu.VMEM((3072, 128), F32),
            pltpu.VMEM((32, 72, 128), F32),
            pltpu.VMEM((16, 144, 128), BF),
            *[pltpu.VMEM((256, 1536), BF)] * 2,
            *[pltpu.VMEM((256, 3072), BF)] * 2,
            *[pltpu.VMEM((16, 156, 128), BF)] * 2,
            pltpu.SemaphoreType.DMA((9,)),
        ],
        compiler_params=PARAMS,
        cost_estimate=pl.CostEstimate(flops=1400000000, bytes_accessed=200000000, transcendentals=0),
        name="adapter_terms",
    )(core.reshape(1), *args)


def pieces_kernel(at, codes, amax, down, up, gate, out, wide):
    core, xi, yh = at[0], at[1], at[2]
    j = yh * 4 + xi
    col = pl.multiple_of(core * 1536 + xi * 384, 128)
    weight = codes[:, pl.ds(col, 384)].astype(F32) * amax[...].astype(F32)
    weight = jnp.where(yh == 0, weight[:24], weight[24:]).astype(BF).astype(F32)
    gates = gate[:, pl.ds(pl.multiple_of(j * 384, 128), 384)].astype(F32)
    for k in range(3):
        lanes = slice(128 * k, 128 * k + 128)
        wide[24 * k : 24 * k + 24] = weight[:, lanes]
        wide[72 + 8 * k : 80 + 8 * k] = gates[:, lanes]

    i = 2 * j + core

    def pick(n, size):
        row = lax.broadcasted_iota(jnp.int32, (n, size), 0)
        col = lax.broadcasted_iota(jnp.int32, (n, size), 1)
        return jnp.where(col == row + n * i, 1.0, 0.0).astype(BF)

    wide[96:99] = nn(pick(3, 48), down[...])
    wide[99:105] = nn(pick(6, 96), up[...])
    for d in range(16):
        out[d] = wide[...].astype(BF)


def pieces(at, codes, amax, down, up, gate):
    return pl.pallas_call(
        pieces_kernel,
        out_shape=jax.ShapeDtypeStruct((16, 105, 128), BF),
        in_specs=[pl.BlockSpec(memory_space=pltpu.SMEM)] + vmem(5),
        out_specs=vmem(1)[0],
        scratch_shapes=[pltpu.VMEM((105, 128), F32)],
        compiler_params=PARAMS,
        name="pieces",
    )(at, codes, amax, down, up, gate)


def spread_kernel(line, features, out_hbm, weight_hbm, wide, maps, pair, out, weight, sems):
    for k in range(3):
        weight[:, :, 128 * k : 128 * k + 128] = line[:, 24 * k : 24 * k + 24]
    copies = fetch([(weight, weight_hbm)], sems.at[pl.ds(0, 1)])
    wide[...] = line[...].astype(F32)
    for z in range(16):
        maps[9 * z : 9 * z + 9] = wide[z, 96:105]
    for k in range(3):
        block = wide[:, 72 + 8 * k : 80 + 8 * k].reshape(128, 128).astype(BF)
        part = nn(features[...], block)
        high = part.astype(BF).astype(F32)
        for h, v in enumerate((high, part - high)):
            for c in range(2):
                for j in range(8):
                    r = 6 * h + 3 * c + k
                    row = v[2 * j + c : 2 * j + c + 1]
                    pair[2 * j, r : r + 1] = row
                    pair[2 * j + 1, r : r + 1] = row
    for d in range(16):
        out[d, :144] = maps[...].astype(BF)
        out[d, 144:] = pair[d].astype(BF)
    copies += fetch([(out, out_hbm)], sems.at[pl.ds(1, 1)])
    for copy in copies:
        copy.wait()


def spread(line, features):
    shapes = ((16, 105, 128), (16, 156, 128), (16, 24, 384))
    return pl.pallas_call(
        spread_kernel,
        out_shape=tuple(jax.ShapeDtypeStruct(s, BF) for s in shapes[1:]),
        in_specs=vmem(2),
        out_specs=tuple(hbm(2)),
        scratch_shapes=[
            pltpu.VMEM(shapes[0], F32),
            pltpu.VMEM((144, 128), F32),
            pltpu.VMEM((16, 12, 128), F32),
            pltpu.VMEM(shapes[1], BF),
            pltpu.VMEM(shapes[2], BF),
            pltpu.SemaphoreType.DMA((2,)),
        ],
        compiler_params=pltpu.CompilerParams(vmem_limit_bytes=14 * 1024 * 1024),
        cost_estimate=pl.CostEstimate(flops=20000000, bytes_accessed=2000000, transcendentals=0),
        name="spread",
    )(line, features)


def per_device(rows, cotangent, codes, amax, down, up, gate_weight, timesteps):
    yh, xi, core, z, yl = (lax.axis_index(a) for a in AXES)
    j = yh * 4 + xi
    y = yh * 2 + yl

    place = jnp.stack([core, xi, yh]).astype(jnp.int32)
    line = pieces(place, codes, amax.reshape(1, 1), down, up.T, gate_weight)
    line = lax.all_to_all(line, "z", 0, 0, tiled=True)
    line, rows_other, cot_other = lax.optimization_barrier(
        (line, other_core(rows), other_core(cotangent))
    )
    k1 = jnp.tile(jnp.arange(4), 4)
    k2 = jnp.repeat(jnp.arange(4), 4)
    bx = xi ^ jnp.where(core == 0, k1, k2)
    by = y ^ jnp.where(core == 0, k2, k1)
    at = jnp.concatenate([bx, (by & 1) * 2 + (by >> 1)]).astype(jnp.int32)

    half_freq = FREQ // 2
    frequency = jnp.exp(-math.log(10000.0) * jnp.arange(half_freq, dtype=F32) / half_freq)
    steps = lax.dynamic_slice(timesteps.reshape(16, 2), (0, z // 8), (16, 1))
    phase = steps.astype(F32) * frequency[None, :]
    features = jnp.concatenate([jnp.cos(phase), jnp.sin(phase)], axis=1).astype(BF)
    features = lax.dynamic_slice(features.reshape(16, 16, 2, 8), (0, 0, yl, 0), (16, 16, 1, 8))
    spread_out, line = spread(line, features.reshape(16, 128))
    got = lax.all_to_all(spread_out, PLANE, 0, 0, tiled=True)
    first = [line] + [lax.ppermute(line, AXES, plane_pairs(k, False)) for k in (1, 2, 3)]
    got, first = lax.optimization_barrier((got, first))
    first = jnp.stack(first)
    second = [first] + [lax.ppermute(first, AXES, plane_pairs(k, True)) for k in (2, 1, 3)]
    second = [second[0], second[2], second[1], second[3]]

    low, low_other, low_grad, gate_own, gate_other, down_all, up_half, terms = adapter_terms(
        core, got, other_core(got), rows, rows_other, cotangent, cot_other
    )
    terms = lax.all_to_all(terms, "z", 0, 0, tiled=True)
    terms = terms.astype(F32).sum(0).astype(BF)

    mixed_other, dx_other, mixed_own, dx_own = products(
        at, core, low_other, gate_other, low, gate_own, low_grad,
        up_half, down_all, *second, rows, rows_other, cotangent, cot_other,
    )
    dx_rest = other_core(dx_other)
    mixed_rest = other_core(mixed_other)
    mixed_rest, dx_rest, terms = lax.optimization_barrier((mixed_rest, dx_rest, terms))
    mixed, dx = finish(core, mixed_own, mixed_rest, dx_own, dx_rest)
    terms = jnp.broadcast_to(terms.reshape(1, 2, 72, 128), (8, 2, 72, 128)).reshape(16, 72, 128)
    terms = lax.all_to_all(terms, PLANE, 0, 0, tiled=True).astype(F32).sum(0)
    rest = other_core(terms)
    terms = jnp.stack([jnp.where(core == 0, terms, rest), jnp.where(core == 0, rest, terms)])
    grad_scale = 131072**-0.5
    down_grad = terms[:, :24].reshape(48, 128) * grad_scale
    up_grad = terms[:, 24:].reshape(96, 128).T * (SCALE * grad_scale)
    return mixed, dx, down_grad, up_grad


def solution(mesh):
    fine = Mesh(mesh.devices.reshape(SIZES), AXES)
    dp, fsdp = ("yh", "x", "core"), ("z", "yl")
    every = dp + fsdp
    in_specs = (
        P(every, None),
        P(every, None),
        P(fsdp, None),
        P(fsdp),
        P(fsdp, None),
        P(None, fsdp),
        P(fsdp, None),
        P(),
    )
    out_specs = (P(every, None), P(every, None), P(fsdp, None), P(None, fsdp))
    return jax.shard_map(
        per_device, mesh=fine, in_specs=in_specs, out_specs=out_specs, check_vma=False
    )
```

```python
import math

import jax
import jax.numpy as jnp
from jax import lax
from jax.experimental import pallas as pl
from jax.experimental.pallas import tpu as pltpu
from jax.sharding import Mesh
from jax.sharding import PartitionSpec as P

FREQ = 256
SCALE = 0.5
AXES = ("yh", "x", "core", "z", "yl")
SIZES = (2, 4, 2, 16, 2)
PLANE = ("yh", "x", "yl")
BF = jnp.bfloat16
F32 = jnp.float32


def index_of(yh, x, c, z, yl):
    return (((yh * 4 + x) * 2 + c) * 16 + z) * 2 + yl


def plane_pairs(k, swap):
    pairs = []
    for yh in range(2):
        for x in range(4):
            for c in range(2):
                for z in range(16):
                    for yl in range(2):
                        tx, ty = x, yh * 2 + yl
                        if (c == 0) != swap:
                            tx ^= k
                        else:
                            ty ^= k
                        pairs.append((index_of(yh, x, c, z, yl), index_of(ty >> 1, tx, c, z, ty & 1)))
    return pairs


def other_core(v):
    return lax.ppermute(v, "core", [(0, 1), (1, 0)])


def nt(a, b):
    return lax.dot_general(a, b, (((1,), (1,)), ((), ())), preferred_element_type=F32)


def nn(a, b):
    return jnp.dot(a, b, preferred_element_type=F32)


STRIPS = [slice(i, i + 256) for i in range(0, 1536, 256)]


def fetch(pairs, sems):
    copies = [pltpu.make_async_copy(a, b, sems.at[i]) for i, (a, b) in enumerate(pairs)]
    for copy in copies:
        copy.start()
    return copies


def products_kernel(
    at, core, low_other, gate_other, low, gate, low_grad,
    up_hbm, down_hbm, t0, t1, t2, t3, rows_hbm, rows_other_hbm, cot_hbm, cot_other_hbm,
    mixed_other_hbm, dx_other_hbm, mixed_hbm, dx_hbm,
    blocks, wm, rows, rows_other, cot, cot_other, branch, branch_other, up, down,
    mixed_other, dx_other, mixed, dx, side_other, side, sems,
):
    half = pl.ds(pl.multiple_of(core[0] * 1536, 128), 1536)
    pairs = [(cot_other_hbm.at[:, half], cot_other), (cot_hbm.at[:, half], cot)]
    pairs += [(down_hbm, down), (up_hbm, up)]
    for k2, t in enumerate((t0, t1, t2, t3)):
        for k1 in range(4):
            b = k2 * 4 + k1
            col = pl.multiple_of(at[b] * 384, 128)
            pairs.append((t.at[k1], blocks.at[:, at[16 + b], :, pl.ds(col, 384)]))
    pairs += [(rows_other_hbm, rows_other), (rows_hbm, rows)]
    copies = fetch(pairs, sems)
    for copy in copies[:4]:
        copy.wait()
    branch_other[...] = (cot_other[...].astype(F32) * gate_other[...]).astype(BF)
    branch[...] = (cot[...].astype(F32) * gate[...]).astype(BF)
    for s in STRIPS:
        dx[:, s] = nt(low_grad[...], down[s, :])
        side_other[:, s] = SCALE * nt(low_other[...], up[s, :])
        side[:, s] = SCALE * nt(low[...], up[s, :])
    for copy in copies[4:20]:
        copy.wait()

    def pack(z, carry):
        part = blocks[z].astype(F32).reshape(96, 1536).astype(BF)
        wm[pl.ds(pl.multiple_of(z * 96, 96), 96), :] = part
        return carry

    lax.fori_loop(0, 16, pack, 0)
    for s in STRIPS:
        dx_other[:, s] = nt(branch_other[...], wm[s, :]).astype(BF)
    out = fetch([(dx_other, dx_other_hbm)], sems.at[pl.ds(22, 1)])
    for copy in copies[20:]:
        copy.wait()
    for s in STRIPS:
        p = nn(rows_other[...], wm[:, s]) + side_other[:, s]
        mixed_other[:, s] = (p * gate_other[:, s]).astype(BF)
    out += fetch([(mixed_other, mixed_other_hbm)], sems.at[pl.ds(23, 1)])
    for s in STRIPS:
        dx[:, s] = nt(branch[...], wm[s, :]) + dx[:, s]
    out += fetch([(dx, dx_hbm)], sems.at[pl.ds(24, 1)])
    for s in STRIPS:
        p = nn(rows[...], wm[:, s]) + side[:, s]
        mixed[:, s] = (p * gate[:, s]).astype(BF)
    out += fetch([(mixed, mixed_hbm.at[:, half])], sems.at[pl.ds(25, 1)])
    for copy in out:
        copy.wait()


def finish_kernel(
    core, mixed_in, mixed_rest_hbm, dx_own_hbm, dx_rest_hbm, mixed_hbm, dx_hbm,
    mixed_rest, dx_own, dx_rest, dx, sems,
):
    rest = pl.ds(pl.multiple_of(1536 - core[0] * 1536, 128), 1536)
    pairs = [(mixed_rest_hbm, mixed_rest), (dx_rest_hbm, dx_rest), (dx_own_hbm, dx_own)]
    copies = fetch(pairs, sems.at[pl.ds(0, 3)])
    copies[0].wait()
    out = fetch([(mixed_rest, mixed_hbm.at[:, rest])], sems.at[pl.ds(3, 1)])
    copies[1].wait()
    copies[2].wait()
    dx[...] = (dx_own[...] + dx_rest[...].astype(F32)).astype(BF)
    out += fetch([(dx, dx_hbm)], sems.at[pl.ds(4, 1)])
    for copy in out:
        copy.wait()


def vmem(n):
    return [pl.BlockSpec(memory_space=pltpu.VMEM)] * n


def adapter_kernel(
    core, got_hbm, got_other_hbm, rows_hbm, rows_other_hbm, cot_hbm, cot_other_hbm,
    low, low_other, low_grad, gate_own, gate_other, down_hbm, up_hbm, terms_hbm,
    wide, parts, down_wide, up_wide, down, up, gates, branch, td, tu, kept, terms,
    rows, rows_other, cot, cot_other, got, got_other, sems,
):
    load = fetch([(got_hbm, got), (got_other_hbm, got_other)], sems.at[pl.ds(7, 2)])
    copies = fetch(
        [(rows_hbm, rows), (rows_other_hbm, rows_other), (cot_hbm, cot), (cot_other_hbm, cot_other)],
        sems.at[pl.ds(0, 4)],
    )
    for copy in load:
        copy.wait()
    first = core[0] == 0
    for s in range(16):
        mine, theirs = got[s].astype(F32), got_other[s].astype(F32)
        wide[s] = mine + theirs
        parts[0] = jnp.where(first, mine, theirs)
        parts[1] = jnp.where(first, theirs, mine)
        j, yl = s // 2, s % 2
        for c in range(2):
            for z in range(16):
                a, b = 96 * z + 48 * yl + 6 * j + 3 * c, 192 * z + 96 * yl + 12 * j + 6 * c
                down_wide[a : a + 3] = parts[c, 9 * z : 9 * z + 3]
                up_wide[b : b + 6] = parts[c, 9 * z + 3 : 9 * z + 9]
    for j in range(8):
        part = wide[2 * j, 144:156] + wide[2 * j + 1, 144:156]
        part = part[:6] + part[6:]
        for r in range(6):
            at = 384 * j + 128 * (r % 3)
            gates[r // 3 : r // 3 + 1, at : at + 128] = part[r : r + 1]
    down[...] = down_wide[...].astype(BF)
    up[...] = up_wide[...].astype(BF)
    at = pl.multiple_of(core[0] * 1536, 128)
    out = fetch([(down, down_hbm), (up.at[pl.ds(at, 1536)], up_hbm)], sems.at[pl.ds(4, 2)])
    gate = jnp.where(first, gates[0:1], gates[1:2])
    gate_own[...] = jnp.where(first, gates[0:1, :1536], gates[1:2, 1536:])
    gate_other[...] = jnp.where(first, gates[1:2, :1536], gates[0:1, 1536:])

    copies[0].wait()
    low[...] = nn(rows[...], down[...]).astype(BF)
    copies[1].wait()
    low_other[...] = nn(rows_other[...], down[...]).astype(BF)
    copies[2].wait()
    branch[:256] = (cot[...].astype(F32) * gate).astype(BF)
    b0 = (SCALE * nn(branch[:256], up[...])).astype(BF)
    low_grad[...] = b0
    copies[3].wait()
    branch[256:] = (cot_other[...].astype(F32) * jnp.where(first, gates[1:2], gates[0:1])).astype(BF)
    b1 = (SCALE * nn(branch[256:], up[...])).astype(BF)
    b0 = b0.astype(F32).T.astype(BF)
    b1 = b1.astype(F32).T.astype(BF)
    a0 = low[...].astype(F32).T.astype(BF)
    a1 = low_other[...].astype(F32).T.astype(BF)
    for i in range(0, 1536, 384):
        s = slice(i, i + 384)
        td[s, :] = (nn(b0, rows[:, s]) + nn(b1, rows_other[:, s])).T
    for i in range(0, 3072, 384):
        s = slice(i, i + 384)
        tu[s, :] = (nn(a0, branch[:256, s]) + nn(a1, branch[256:, s])).T

    def put(h):
        kept[:, :24] = td[...].reshape(32, 2, 24, 128)[:, h]
        kept[:, 24:] = tu[...].reshape(32, 2, 48, 128)[:, h]

    @pl.when(first)
    def _():
        put(0)

    @pl.when(jnp.logical_not(first))
    def _():
        put(1)

    terms[...] = kept[...].reshape(16, 144, 128).astype(BF)
    out += fetch([(terms, terms_hbm)], sems.at[pl.ds(6, 1)])
    for copy in out:
        copy.wait()


PARAMS = pltpu.CompilerParams(vmem_limit_bytes=60 * 1024 * 1024)
HALF = 256 * 1536 * 1536 * 2


def hbm(n):
    return [pl.BlockSpec(memory_space=pltpu.HBM)] * n


def products(at, core, *args):
    half = jax.ShapeDtypeStruct((256, 1536), BF)
    return pl.pallas_call(
        products_kernel,
        out_shape=(
            half,
            half,
            jax.ShapeDtypeStruct((256, 3072), BF),
            jax.ShapeDtypeStruct((256, 1536), F32),
        ),
        in_specs=[pl.BlockSpec(memory_space=pltpu.SMEM)] * 2 + vmem(5) + hbm(10),
        out_specs=tuple(hbm(4)),
        scratch_shapes=[
            pltpu.VMEM((16, 4, 24, 1536), BF),
            pltpu.VMEM((1536, 1536), BF),
            *[pltpu.VMEM((256, 1536), BF)] * 6,
            *[pltpu.VMEM((1536, 128), BF)] * 2,
            *[pltpu.VMEM((256, 1536), BF)] * 3,
            *[pltpu.VMEM((256, 1536), F32)] * 3,
            pltpu.SemaphoreType.DMA((26,)),
        ],
        compiler_params=PARAMS,
        cost_estimate=pl.CostEstimate(flops=4 * HALF, bytes_accessed=200000000, transcendentals=0),
        name="products",
    )(at, core.reshape(1), *args)


def finish(core, *args):
    return pl.pallas_call(
        finish_kernel,
        out_shape=(jax.ShapeDtypeStruct((256, 3072), BF), jax.ShapeDtypeStruct((256, 1536), BF)),
        in_specs=[pl.BlockSpec(memory_space=pltpu.SMEM)] + hbm(4),
        out_specs=tuple(hbm(2)),
        input_output_aliases={1: 0},
        scratch_shapes=[
            pltpu.VMEM((256, 1536), BF),
            pltpu.VMEM((256, 1536), F32),
            *[pltpu.VMEM((256, 1536), BF)] * 2,
            pltpu.SemaphoreType.DMA((5,)),
        ],
        compiler_params=PARAMS,
        cost_estimate=pl.CostEstimate(flops=1000000, bytes_accessed=7000000, transcendentals=0),
        name="finish",
    )(core.reshape(1), *args)


def adapter_terms(core, *args):
    def out(*shape):
        return jax.ShapeDtypeStruct(shape, BF)

    thin, row = out(256, 128), jax.ShapeDtypeStruct((1, 1536), F32)
    tall = out(1536, 128)
    return pl.pallas_call(
        adapter_kernel,
        out_shape=(thin, thin, thin, row, row, tall, tall, out(16, 144, 128)),
        in_specs=[pl.BlockSpec(memory_space=pltpu.SMEM)] + hbm(6),
        out_specs=tuple(vmem(5) + hbm(3)),
        scratch_shapes=[
            pltpu.VMEM((16, 156, 128), F32),
            pltpu.VMEM((2, 156, 128), F32),
            pltpu.VMEM((1536, 128), F32),
            pltpu.VMEM((3072, 128), F32),
            pltpu.VMEM((1536, 128), BF),
            pltpu.VMEM((3072, 128), BF),
            pltpu.VMEM((2, 3072), F32),
            pltpu.VMEM((512, 3072), BF),
            pltpu.VMEM((1536, 128), F32),
            pltpu.VMEM((3072, 128), F32),
            pltpu.VMEM((32, 72, 128), F32),
            pltpu.VMEM((16, 144, 128), BF),
            *[pltpu.VMEM((256, 1536), BF)] * 2,
            *[pltpu.VMEM((256, 3072), BF)] * 2,
            *[pltpu.VMEM((16, 156, 128), BF)] * 2,
            pltpu.SemaphoreType.DMA((9,)),
        ],
        compiler_params=PARAMS,
        cost_estimate=pl.CostEstimate(flops=1400000000, bytes_accessed=200000000, transcendentals=0),
        name="adapter_terms",
    )(core.reshape(1), *args)


def pieces_kernel(at, codes, amax, down, up, gate, out, wide):
    core, xi, yh = at[0], at[1], at[2]
    j = yh * 4 + xi
    col = pl.multiple_of(core * 1536 + xi * 384, 128)
    weight = codes[:, pl.ds(col, 384)].astype(F32) * amax[...].astype(F32)
    weight = jnp.where(yh == 0, weight[:24], weight[24:]).astype(BF).astype(F32)
    gates = gate[:, pl.ds(pl.multiple_of(j * 384, 128), 384)].astype(F32)
    gates = jnp.where(core == 0, gates[:4], gates[4:])
    for k in range(3):
        lanes = slice(128 * k, 128 * k + 128)
        wide[24 * k : 24 * k + 24] = weight[:, lanes]
        wide[72 + 4 * k : 76 + 4 * k] = gates[:, lanes]

    i = 2 * j + core

    def pick(n, size):
        row = lax.broadcasted_iota(jnp.int32, (n, size), 0)
        col = lax.broadcasted_iota(jnp.int32, (n, size), 1)
        return jnp.where(col == row + n * i, 1.0, 0.0).astype(BF)

    wide[84:87] = nn(pick(3, 48), down[...])
    wide[87:93] = nn(pick(6, 96), up[...])
    for d in range(16):
        out[d] = wide[...].astype(BF)


def pieces(at, codes, amax, down, up, gate):
    return pl.pallas_call(
        pieces_kernel,
        out_shape=jax.ShapeDtypeStruct((16, 93, 128), BF),
        in_specs=[pl.BlockSpec(memory_space=pltpu.SMEM)] + vmem(5),
        out_specs=vmem(1)[0],
        scratch_shapes=[pltpu.VMEM((93, 128), F32)],
        compiler_params=PARAMS,
        name="pieces",
    )(at, codes, amax, down, up, gate)


def spread_kernel(line, features, out_hbm, weight_hbm, wide, maps, blocks, pair, out, weight, sems):
    for k in range(3):
        weight[:, :, 128 * k : 128 * k + 128] = line[:, 24 * k : 24 * k + 24]
    copies = fetch([(weight, weight_hbm)], sems.at[pl.ds(0, 1)])
    wide[...] = line[...].astype(F32)
    for z in range(16):
        maps[9 * z : 9 * z + 9] = wide[z, 84:93]
        for k in range(3):
            blocks[k, 4 * z : 4 * z + 4] = wide[z, 72 + 4 * k : 76 + 4 * k]
    for k in range(3):
        part = nn(features[...], blocks[k].astype(BF))
        high = part.astype(BF).astype(F32)
        for h, v in enumerate((high, part - high)):
            for c in range(2):
                for j in range(8):
                    r = 6 * h + 3 * c + k
                    row = v[2 * j + c : 2 * j + c + 1]
                    pair[2 * j, r : r + 1] = row
                    pair[2 * j + 1, r : r + 1] = row
    for d in range(16):
        out[d, :144] = maps[...].astype(BF)
        out[d, 144:] = pair[d].astype(BF)
    copies += fetch([(out, out_hbm)], sems.at[pl.ds(1, 1)])
    for copy in copies:
        copy.wait()


def spread(line, features):
    shapes = ((16, 93, 128), (16, 156, 128), (16, 24, 384))
    return pl.pallas_call(
        spread_kernel,
        out_shape=tuple(jax.ShapeDtypeStruct(s, BF) for s in shapes[1:]),
        in_specs=vmem(2),
        out_specs=tuple(hbm(2)),
        scratch_shapes=[
            pltpu.VMEM(shapes[0], F32),
            pltpu.VMEM((144, 128), F32),
            pltpu.VMEM((3, 64, 128), F32),
            pltpu.VMEM((16, 12, 128), F32),
            pltpu.VMEM(shapes[1], BF),
            pltpu.VMEM(shapes[2], BF),
            pltpu.SemaphoreType.DMA((2,)),
        ],
        compiler_params=pltpu.CompilerParams(vmem_limit_bytes=14 * 1024 * 1024),
        cost_estimate=pl.CostEstimate(flops=20000000, bytes_accessed=2000000, transcendentals=0),
        name="spread",
    )(line, features)


def per_device(rows, cotangent, codes, amax, down, up, gate_weight, timesteps):
    yh, xi, core, z, yl = (lax.axis_index(a) for a in AXES)
    j = yh * 4 + xi
    y = yh * 2 + yl

    place = jnp.stack([core, xi, yh]).astype(jnp.int32)
    line = pieces(place, codes, amax.reshape(1, 1), down, up.T, gate_weight)
    line = lax.all_to_all(line, "z", 0, 0, tiled=True)
    line, rows_other, cot_other = lax.optimization_barrier(
        (line, other_core(rows), other_core(cotangent))
    )
    k1 = jnp.tile(jnp.arange(4), 4)
    k2 = jnp.repeat(jnp.arange(4), 4)
    bx = xi ^ jnp.where(core == 0, k1, k2)
    by = y ^ jnp.where(core == 0, k2, k1)
    at = jnp.concatenate([bx, (by & 1) * 2 + (by >> 1)]).astype(jnp.int32)

    half_freq = FREQ // 2
    frequency = jnp.exp(-math.log(10000.0) * jnp.arange(half_freq, dtype=F32) / half_freq)
    steps = lax.dynamic_slice(timesteps.reshape(16, 2), (0, z // 8), (16, 1))
    phase = steps.astype(F32) * frequency[None, :]
    features = jnp.concatenate([jnp.cos(phase), jnp.sin(phase)], axis=1).astype(BF)
    features = features.reshape(16, 16, 2, 2, 4)
    features = lax.dynamic_slice(features, (0, 0, yl, core, 0), (16, 16, 1, 1, 4))
    spread_out, line = spread(line, features.reshape(16, 64))
    got = lax.all_to_all(spread_out, PLANE, 0, 0, tiled=True)
    first = [line] + [lax.ppermute(line, AXES, plane_pairs(k, False)) for k in (1, 2, 3)]
    got, first = lax.optimization_barrier((got, first))
    first = jnp.stack(first)
    second = [first] + [lax.ppermute(first, AXES, plane_pairs(k, True)) for k in (2, 1, 3)]
    second = [second[0], second[2], second[1], second[3]]

    low, low_other, low_grad, gate_own, gate_other, down_all, up_half, terms = adapter_terms(
        core, got, other_core(got), rows, rows_other, cotangent, cot_other
    )
    terms = lax.all_to_all(terms, "z", 0, 0, tiled=True)
    terms = terms.astype(F32).sum(0).astype(BF)

    mixed_other, dx_other, mixed_own, dx_own = products(
        at, core, low_other, gate_other, low, gate_own, low_grad,
        up_half, down_all, *second, rows, rows_other, cotangent, cot_other,
    )
    dx_rest = other_core(dx_other)
    mixed_rest = other_core(mixed_other)
    mixed_rest, dx_rest, terms = lax.optimization_barrier((mixed_rest, dx_rest, terms))
    mixed, dx = finish(core, mixed_own, mixed_rest, dx_own, dx_rest)
    terms = jnp.broadcast_to(terms.reshape(1, 2, 72, 128), (8, 2, 72, 128)).reshape(16, 72, 128)
    terms = lax.all_to_all(terms, PLANE, 0, 0, tiled=True).astype(F32).sum(0)
    rest = other_core(terms)
    terms = jnp.stack([jnp.where(core == 0, terms, rest), jnp.where(core == 0, rest, terms)])
    grad_scale = 131072**-0.5
    down_grad = terms[:, :24].reshape(48, 128) * grad_scale
    up_grad = terms[:, 24:].reshape(96, 128).T * (SCALE * grad_scale)
    return mixed, dx, down_grad, up_grad


def solution(mesh):
    fine = Mesh(mesh.devices.reshape(SIZES), AXES)
    dp, fsdp = ("yh", "x", "core"), ("z", "yl")
    every = dp + fsdp
    in_specs = (
        P(every, None),
        P(every, None),
        P(fsdp, None),
        P(fsdp),
        P(fsdp, None),
        P(None, fsdp),
        P(fsdp, None),
        P(),
    )
    out_specs = (P(every, None), P(every, None), P(fsdp, None), P(None, fsdp))
    return jax.shard_map(
        per_device, mesh=fine, in_specs=in_specs, out_specs=out_specs, check_vma=False
    )
```
